512 devices in a mesh: item: 8 (over z), seq: 64 (over x, y, core).
Axes of the slice: x: 4, y: 8, z: 8, core: 2. Of those that a mesh axis runs over, the one named last changes fastest.
Arguments:
- item_states: bfloat16 [16384, 2048], P(('item', 'seq')), may hold values from -6 to 6
- item_gain: float32 [2048], replicated, may hold values from 0.25 to 1.75
- hist_ids: int32 [32768], P('seq'), may hold values from 0 to 16383, as said below
- lengths: int32 [8], replicated, may hold values from 1 to 4096, as said below
- attn_gain: float32 [2048], replicated, may hold values from 0.25 to 1.75
- w_q: bfloat16 [2048, 2048], P(None, 'item')
- w_kv: bfloat16 [2048, 2, 1024], P(None, None, 'item')
- q_gain: float32 [128], replicated
- k_gain: float32 [128], replicated
- w_out: bfloat16 [2048, 2048], P('item'), may hold values from -0.125 to 0.125
Outputs:
- mixed: bfloat16 [32768, 2048], P('seq', 'item')
The draws below stay inside these ranges and needn't reach their ends.
Inputs may be any that keep to these rules, and one draw needn't show every extreme that they name: `hist_ids`: among the 512 slots of one index of seq, at most 2 refer to items of one block of 32 consecutive ids, and in every such group of slots some block has exactly 2. `lengths`: some user has the full 4096 slots.
All inputs are finite; a program needn't handle non-finite values.
Results may differ from the reference program's by a relative error of at most 0.014.
Values may be sent and summed in bfloat16 or wider, within the bound.
A program may use at most 64 MiB of HBM per device.

```python
import jax
import jax.numpy as jnp
from jax import lax

D = 2048
HEADS = 16
KVH = 8
HD = 128
LEN = 4096
ROWS_DEV = 512
IT_DEV = 32
ITEMS = 16384
ROWS = 32768
SEQS = 8
CAP = 2
N_ITEM = 8
N_SEQ = 64


def shared_query(key):
    return jax.random.normal(key, (D, HEADS * HD), jnp.float32)


def draw_hist_ids(key, part):
    key = jax.random.fold_in(key, 11)
    owners = N_ITEM * N_SEQ

    def one_block(block_key):
        first, second, third, fourth = jax.random.split(block_key, 4)
        order = jax.random.permutation(first, owners)
        seats = jax.random.permutation(second, (owners - 1) * CAP)[:ROWS_DEV - CAP]
        picks = jnp.concatenate([jnp.zeros((CAP,), jnp.int32), 1 + seats // CAP])
        owner = jax.random.permutation(third, order[picks])
        inner = jax.random.randint(fourth, (ROWS_DEV,), 0, IT_DEV)
        return (owner * IT_DEV + inner).astype(jnp.int32)
    return jax.vmap(one_block)(jax.random.split(key, N_SEQ)).reshape(ROWS)


def draw_lengths(key, part):
    key = jax.random.fold_in(key, 12)
    first, second = jax.random.split(key)
    drawn = jax.random.randint(first, (SEQS,), 1, LEN + 1)
    where_full = jax.random.randint(second, (), 0, SEQS)
    return drawn.at[where_full].set(LEN).astype(jnp.int32)


def draw_w_q(key, part):
    base = shared_query(key)
    return (base * D ** (-0.5)).astype(jnp.bfloat16)


def draw_w_kv(key, part):
    key = jax.random.fold_in(key, 14)
    fresh = jax.random.normal(key, (D, 2, KVH * HD), jnp.float32)
    both = fresh
    return (both * D ** (-0.5)).astype(jnp.bfloat16)


def draw_q_gain(key, part):
    key = jax.random.fold_in(key, 15)
    return jax.random.uniform(key, (HD,), jnp.float32, 0.7, 1.5)


def draw_k_gain(key, part):
    key = jax.random.fold_in(key, 16)
    return jax.random.uniform(key, (HD,), jnp.float32, 0.7, 1.5)


def block_scale(own_key, extent, cuts, smallest, high):
    level, own = 1.0, jax.random.fold_in(own_key, 6)
    for dim, blocks in cuts:
        steps = jnp.exp(jax.random.uniform(jax.random.fold_in(own, dim), (blocks,), jnp.float32, smallest / len(cuts), high / len(cuts)))
        level = level * jnp.repeat(steps, extent[dim] // blocks).reshape([-1 if axis == dim else 1 for axis in range(len(extent))])
    return level


def gaussian(own_key, shape, width, most, shards=(), kind=jnp.bfloat16):
    values = jax.random.normal(own_key, shape, jnp.float32) * width
    if len(shards) > 0:
        values = block_scale(own_key, shape, shards, -0.22, 0.18) * values
    return jnp.clip(values, min=-most, max=most).astype(kind)


def setup_inputs(seed: int = 0) -> dict:
    key_of = jax.random.split(jax.random.key(seed), 11)
    item_states = gaussian(key_of[0], (ITEMS, D), 1.0, 6.0, ((0, 512),))
    item_gain = jnp.clip(1.0 + 0.15 * jax.random.normal(key_of[1], (D,), jnp.float32), 0.25, 1.75)
    hist_ids = draw_hist_ids(jax.random.fold_in(key_of[10], 71), 0)
    lengths = draw_lengths(jax.random.fold_in(key_of[10], 71), 0)
    attn_gain = jnp.clip(1.0 + 0.15 * jax.random.normal(key_of[4], (D,), jnp.float32), 0.25, 1.75)
    w_q = draw_w_q(jax.random.fold_in(key_of[10], 71), 0)
    w_kv = draw_w_kv(jax.random.fold_in(key_of[10], 71), 0)
    q_gain = draw_q_gain(jax.random.fold_in(key_of[10], 71), 0)
    k_gain = draw_k_gain(jax.random.fold_in(key_of[10], 71), 0)
    w_out = gaussian(key_of[9], (HEADS * HD, D), (HEADS * HD) ** -0.5, 0.125, ((0, 8),))
    return dict(item_states=item_states, item_gain=item_gain, hist_ids=hist_ids, lengths=lengths, attn_gain=attn_gain, w_q=w_q, w_kv=w_kv, q_gain=q_gain, k_gain=k_gain, w_out=w_out)


def rms(x, gain):
    return x * lax.rsqrt(lax.optimization_barrier(jnp.mean(x * x, axis=-1, keepdims=True)) + 1e-06) * gain

def reference(item_states, item_gain, hist_ids, lengths, attn_gain, w_q, w_kv, q_gain, k_gain, w_out):
    group = HEADS // KVH
    embed = rms(item_states.astype(jnp.float32), item_gain).astype(jnp.bfloat16)
    hist = jnp.take(embed, hist_ids, axis=0)
    normed = rms(hist.astype(jnp.float32), attn_gain).astype(jnp.bfloat16)
    query = jnp.dot(normed, w_q, preferred_element_type=jnp.float32).reshape(ROWS, KVH, group, HD)
    query = rms(query, q_gain).astype(jnp.bfloat16)
    pairs = jnp.dot(normed, w_kv.reshape(D, 2 * KVH * HD), preferred_element_type=jnp.float32)
    pairs = pairs.reshape(ROWS, 2, KVH, HD)
    keys = rms(pairs[:, 0], k_gain).astype(jnp.bfloat16)
    values = pairs[:, 1].astype(jnp.bfloat16)
    scale = 1.0 / HD ** 0.5
    positions = jnp.arange(LEN, dtype=jnp.int32)

    def one_user(index):
        start = (index * LEN).astype(jnp.int32)
        qs = lax.dynamic_slice_in_dim(query, start, LEN, 0)
        ks = lax.dynamic_slice_in_dim(keys, start, LEN, 0)
        vs = lax.dynamic_slice_in_dim(values, start, LEN, 0)
        length = lengths[index]
        allowed = (positions[None, :] <= positions[:, None]) & (positions[None, :] < length)

        def one_head(head):
            qh = qs[:, head].astype(jnp.float32)
            kh = ks[:, head].astype(jnp.float32)
            vh = vs[:, head].astype(jnp.float32)
            score = jnp.einsum('igc,jc->gij', qh, kh) * scale
            score = jnp.where(allowed[None], score, -1e+30)
            top = lax.optimization_barrier(jnp.max(score, axis=-1, keepdims=True))
            weights = jnp.where(allowed[None], jnp.exp(score - top), 0.0)
            total = lax.optimization_barrier(jnp.sum(weights, axis=-1))
            rounded = weights.astype(jnp.bfloat16).astype(jnp.float32)
            out = jnp.einsum('gij,jc->gic', rounded, vh) / total[..., None]
            return out.astype(jnp.bfloat16)
        heads = lax.map(one_head, jnp.arange(KVH, dtype=jnp.int32))
        return jnp.transpose(heads, (2, 0, 1, 3)).reshape(LEN, HEADS * HD)
    attn = lax.map(one_user, jnp.arange(SEQS, dtype=jnp.int32)).reshape(ROWS, HEADS * HD)
    proj = jnp.dot(attn, w_out, preferred_element_type=jnp.float32)
    row_len = lengths[jnp.arange(ROWS, dtype=jnp.int32) // LEN]
    valid = jnp.arange(ROWS, dtype=jnp.int32) % LEN < row_len
    mixed = hist.astype(jnp.float32) + jnp.where(valid[:, None], proj, 0.0)
    return mixed.astype(jnp.bfloat16)
```

```python
import functools

import jax
import jax.numpy as jnp
from jax import lax
from jax.experimental import pallas as pl
from jax.experimental.pallas import tpu as pltpu
from jax.sharding import PartitionSpec as P

HD = 128
LEN = 4096
CORES = 2
NY = 8
F32, BF16, I32 = jnp.float32, jnp.bfloat16, jnp.int32
VMEM_LIMIT = 48 * 1024 * 1024


def rms(x, gain):
    return x * lax.rsqrt(jnp.mean(x * x, axis=-1, keepdims=True) + 1e-06) * gain


def iota(shape, dim):
    return lax.broadcasted_iota(I32, shape, dim)


def onehot(mask):
    return jnp.where(mask, 1.0, 0.0).astype(BF16)


def dot(a, b):
    return jnp.dot(a, b, preferred_element_type=F32)


def signal(sem, **where):
    pl.semaphore_signal(sem, inc=1, device_id=where, device_id_type=pl.DeviceIdType.MESH)


def remote(src, dst, send, recv, **where):
    return pltpu.make_async_remote_copy(
        src_ref=src, dst_ref=dst, send_sem=send, recv_sem=recv,
        device_id=where, device_id_type=pl.DeviceIdType.MESH,
    )


class ZRing:
    def __init__(self, buf, send, recv, n):
        self.buf, self.send, self.recv, self.n = buf, send, recv, n
        self.me = lax.axis_index("item")

    def live(self, way, hop, half):
        return hop < self.n // 2 or (hop == self.n // 2 and half == way)

    def copy(self, way, hop, half, shard):
        step = 1 if way == 0 else self.n - 1
        piece = self.buf.at[shard * 2 + half]
        at = (way, hop - 1, half)
        return remote(
            piece, piece, self.send.at[at], self.recv.at[at],
            item=lax.rem(self.me + step, self.n),
        )

    def shard(self, way, hop):
        return lax.rem(self.me + (self.n - hop if way == 0 else hop), self.n)

    def start(self, hop):
        for half in range(2):
            self.start_half(hop, half)

    def start_half(self, hop, half):
        for way in range(2):
            if self.live(way, hop, half):
                self.copy(way, hop, half, self.shard(way, hop - 1)).start()

    def land(self, hop):
        for half in range(2):
            for way in range(2):
                if self.live(way, hop, half):
                    self.copy(way, hop, half, self.shard(way, hop)).wait_recv()
                    if self.live(way, hop + 1, half):
                        self.copy(way, hop + 1, half, self.shard(way, hop)).start()

    def drain(self):
        for hop in range(1, self.n // 2 + 1):
            for half in range(2):
                for way in range(2):
                    if self.live(way, hop, half):
                        self.copy(way, hop, half, self.shard(way, hop - 1)).wait_send()


def rank_of(ids_row, ids_col, per_dev, n_seq, axis):
    rows = ids_row.shape[1]
    owner_row = (ids_row // per_dev) & (n_seq - 1)
    owner_col = (ids_col // per_dev) & (n_seq - 1)
    lane, sub = iota((rows, rows), 1), iota((rows, rows), 0)
    if axis == 0:
        same = (owner_col == owner_row) & (sub < lane)
        less = owner_col < owner_row
    else:
        same = (owner_col == owner_row) & (lane < sub)
        less = owner_row < owner_col
    within = jnp.sum(jnp.where(same, 1.0, 0.0), axis=axis, keepdims=True).astype(I32)
    before = jnp.sum(jnp.where(less, 1.0, 0.0), axis=axis, keepdims=True).astype(I32)
    return before + within, within


def fetch_kernel(
    n_item, n_seq, ny, ids_row_ref, ids_col_ref, states_ref, gain_ref, out_ref,
    table, id_a, id_b, id_c, id_d, found, mid, turned, final,
    z_send, z_recv, iy_send, iy_recv, ix_send, ix_recv, rx_send, rx_recv, ry_send, ry_recv,
):
    nq = n_seq // ny
    me = lax.axis_index("item")
    my_seq = lax.axis_index("seq")
    my_core = lax.rem(my_seq, CORES)
    my_y = lax.rem(my_seq // CORES, ny)
    my_x = my_seq // (CORES * ny)
    my_q = my_x * CORES + my_core
    per_dev, width = states_ref.shape
    rows = ids_row_ref.shape[1]
    share = rows // n_item

    def along_y(y):
        return (my_x * ny + y) * CORES + my_core

    def along_q(q):
        return ((q // CORES) * ny + my_y) * CORES + lax.rem(q, CORES)

    def y_plus(d):
        return lax.rem(my_y + d, ny)

    def q_plus(d):
        return lax.rem(my_q + d, nq)

    barrier = pltpu.get_barrier_semaphore()
    for step in (1, n_item - 1):
        signal(barrier, item=lax.rem(me + step, n_item))
    for d in range(1, ny):
        signal(barrier, seq=along_y(y_plus(d)))
    for d in range(1, nq):
        signal(barrier, seq=along_q(q_plus(d)))

    embed = rms(states_ref[...].astype(F32), gain_ref[...]).astype(BF16)
    half = per_dev // 2
    table[pl.ds(me * 2, 2)] = embed.reshape(2, half, width)
    pl.semaphore_wait(barrier, 2 + (ny - 1) + (nq - 1))

    ring = ZRing(table, z_send, z_recv, n_item)
    ring.start(1)

    ids_row = ids_row_ref[...]
    rank, within = rank_of(ids_row, ids_col_ref[...], per_dev, n_seq, 0)
    owner = ids_row // per_dev
    owner_seq = owner & (n_seq - 1)
    source_y = (owner_seq // CORES) & (ny - 1)
    source_q = (owner_seq // (CORES * ny)) * CORES + (owner_seq & (CORES - 1))
    item = (owner // n_seq) * per_dev + (ids_row & (per_dev - 1)) + 1
    mine = (rank & (n_item - 1)) == me
    copy_no = within // n_item
    place = jnp.where(mine, source_y * nq + source_q, -1)
    asked = []
    for sub in range(2):
        hit = (iota((ny * nq, rows), 0) == place) & (copy_no == sub)
        asked.append(jnp.sum(jnp.where(hit, item.astype(F32), 0.0), axis=1, keepdims=True).astype(I32))
    lanes = iota((ny * nq, 128), 1)
    id_a[...] = jnp.where(lanes == 0, asked[0], jnp.where(lanes == 1, asked[1], 0)).reshape(ny, nq, 128)

    def ids_y(d, y_from, y_to):
        return remote(
            id_a.at[y_to], id_b.at[y_from], iy_send.at[d - 1], iy_recv.at[d - 1], seq=along_y(y_to)
        )

    def ids_q(d, q_from, q_to):
        return remote(
            id_c.at[q_to], id_d.at[q_from], ix_send.at[d - 1], ix_recv.at[d - 1], seq=along_q(q_to)
        )

    for d in range(1, ny):
        ids_y(d, my_y, y_plus(d)).start()
    id_b[my_y] = id_a[my_y]
    ring.land(1)
    for d in range(1, ny):
        ids_y(d, y_plus(ny - d), my_y).wait_recv()
    for q in range(nq):
        id_c[q] = id_b[:, q, :]
    for d in range(1, nq):
        ids_q(d, my_q, q_plus(d)).start()
    id_d[my_q] = id_c[my_q]
    for hop in range(2, n_item // 2):
        ring.land(hop)
    spot = jnp.where(mine, rank // n_item, -1)
    pick_a = onehot(iota((share, rows), 0) == spot)
    pick_b = onehot(iota((ny * nq * 2, rows), 0) == jnp.where(mine, place * 2 + copy_no, -1))
    pick = lax.dot_general(pick_a, pick_b, (((1,), (1,)), ((), ())), preferred_element_type=F32).astype(BF16)
    for d in range(1, nq):
        ids_q(d, q_plus(nq - d), my_q).wait_recv()
    wanted = id_d[...].reshape(nq * ny, 128)
    items = iota((nq * ny, n_item * per_dev), 1) + 1
    choose = jnp.stack(
        [jnp.where(wanted[:, sub:sub + 1] == items, 1.0, 0.0).reshape(nq, ny, n_item * per_dev) for sub in range(2)],
        axis=1,
    ).reshape(nq * 2 * ny, n_item * per_dev).astype(BF16)
    if n_item > 2:
        ring.land(n_item // 2)
    else:
        pass

    parts = found.shape[0]
    cols = width // parts
    to, frm = iota((ny * nq * 2, nq * 2 * ny), 0), iota((ny * nq * 2, nq * 2 * ny), 1)
    to_y, to_q, to_sub = to // (nq * 2), (to // 2) % nq, to % 2
    turn = onehot(frm == (to_q * 2 + to_sub) * ny + to_y)

    def rows_q(part, d, q_from, q_to):
        return remote(
            found.at[part, q_to], mid.at[part, q_from],
            rx_send.at[part, d - 1], rx_recv.at[part, d - 1], seq=along_q(q_to),
        )

    def rows_y(part, d, y_from, y_to):
        return remote(
            turned.at[part, y_to], final.at[part, y_from],
            ry_send.at[part, d - 1], ry_recv.at[part, d - 1], seq=along_y(y_to),
        )

    for part in range(parts):
        span = slice(part * cols, (part + 1) * cols)
        source = table[:, :, span].reshape(n_item * per_dev, cols)
        found[part] = dot(choose, source).astype(BF16).reshape(nq, 2 * ny, cols)
        for d in range(1, nq):
            rows_q(part, d, my_q, q_plus(d)).start()
        mid[part, my_q] = found[part, my_q]
    for part in range(parts):
        for d in range(1, nq):
            rows_q(part, d, q_plus(nq - d), my_q).wait_recv()
        turned[part] = dot(turn, mid[part].reshape(nq * 2 * ny, cols)).astype(BF16).reshape(ny, 2 * nq, cols)
        for d in range(1, ny):
            rows_y(part, d, my_y, y_plus(d)).start()
        final[part, my_y] = turned[part, my_y]
    for part in range(parts):
        for d in range(1, ny):
            rows_y(part, d, y_plus(ny - d), my_y).wait_recv()
        out_ref[:, part * cols:(part + 1) * cols] = dot(
            pick, final[part].reshape(ny * 2 * nq, cols)
        ).astype(BF16)

    ring.drain()
    for d in range(1, ny):
        ids_y(d, my_y, y_plus(d)).wait_send()
    for d in range(1, nq):
        ids_q(d, my_q, q_plus(d)).wait_send()
    for part in range(parts):
        for d in range(1, nq):
            rows_q(part, d, my_q, q_plus(d)).wait_send()
        for d in range(1, ny):
            rows_y(part, d, my_y, y_plus(d)).wait_send()


def attend_kernel(
    n_item, n_seq, per_dev, ids_row_ref, ids_col_ref, len_ref, rows_ref, again_ref, wq_ref, wkv_ref,
    qg_ref, kg_ref, attn_ref, res_ref,
    every, ranked, query, kv, acc, top, total,
    z_send, z_recv, lane_send, lane_recv, pair_send, pair_recv,
):
    me = lax.axis_index("item")
    my_seq = lax.axis_index("seq")
    rows = ids_row_ref.shape[1]
    share, width = rows_ref.shape
    span = LEN // rows
    chips = span // CORES
    core = lax.rem(my_seq, CORES)
    chip = lax.rem(my_seq // CORES, chips)
    other = 1 - core
    base = lax.rem(my_seq, span) * rows
    length = len_ref[my_seq // span]
    q_cols = wq_ref.shape[1]
    group = q_cols // HD
    cols = width // n_item
    sibling = my_seq + 1 - 2 * core

    barrier = pltpu.get_barrier_semaphore()
    for step in (1, n_item - 1):
        signal(barrier, item=lax.rem(me + step, n_item))
    signal(barrier, seq=sibling)

    @pl.when(chip > 0)
    def _():
        signal(barrier, seq=my_seq - CORES)

    @pl.when(chip < chips - 1)
    def _():
        signal(barrier, seq=my_seq + CORES)

    every[pl.ds(me * 2, 2)] = rows_ref[...].reshape(2, share // 2, width)
    ahead = (2 * chips - 2 - chip) // chips
    behind = (chip + chips - 1) // chips
    pl.semaphore_wait(barrier, 3 + ahead + behind)

    ring = ZRing(every, z_send, z_recv, n_item)
    ring.start(1)

    def project(shards):
        x = jnp.concatenate([every[pl.ds(j * 2, 2)].reshape(share, width) for j in shards], axis=0)
        normed = rms(x.astype(F32), again_ref[...]).astype(BF16)
        q = dot(normed, wq_ref[...])
        pair = dot(normed, wkv_ref[...])
        pieces = [rms(q[:, g * HD:(g + 1) * HD], qg_ref[...]).astype(BF16) for g in range(group)]
        pieces.append(rms(pair[:, :HD], kg_ref[...]).astype(BF16))
        pieces.append(pair[:, HD:].astype(BF16))
        for at, j in enumerate(shards):
            here = pl.ds(pl.multiple_of(j * share, share), share)
            for c, piece in enumerate(pieces):
                ranked[here, c * HD:(c + 1) * HD] = piece[at * share:(at + 1) * share]
            mine = every[pl.ds(j * 2, 2), :, pl.ds(pl.multiple_of(me * cols, cols), cols)]
            ranked[here, q_cols + 2 * HD:] = mine.reshape(share, cols)

    project([me])
    for hop in range(1, n_item // 2):
        ring.land(hop)
        project([ring.shard(0, hop), ring.shard(1, hop)])
    ring.land(n_item // 2)
    project([ring.shard(0, n_item // 2)])

    rank, _ = rank_of(ids_row_ref[...], ids_col_ref[...], per_dev, n_seq, 1)
    goal = (rank & (n_item - 1)) * share + rank // n_item
    order = onehot(goal == iota((rows, rows), 1))
    placed = dot(order, ranked[...]).astype(BF16)
    for g in range(group):
        query[g * rows:(g + 1) * rows] = placed[:, g * HD:(g + 1) * HD]
    kv[core] = placed[:, q_cols:q_cols + 2 * HD].reshape(2, rows // 2, 2 * HD)
    res_ref[...] = placed[:, q_cols + 2 * HD:]

    def lane_copy(hop, half):
        return remote(
            kv.at[(hop - 1) * 2 + core, half], kv.at[hop * 2 + core, half],
            lane_send.at[hop - 1, half], lane_recv.at[hop - 1, half], seq=my_seq + CORES,
        )

    def pair_copy(hop, half, lane):
        return remote(
            kv.at[hop * 2 + lane, half], kv.at[hop * 2 + lane, half],
            pair_send.at[hop, half], pair_recv.at[hop, half], seq=sibling,
        )

    not_last = chip < chips - 1

    @pl.when(not_last)
    def _():
        for half in range(2):
            lane_copy(1, half).start()

    @pl.when(core == 0)
    def _():
        for half in range(2):
            pair_copy(0, half, 0).start()

    scale = 1.4426950408889634 / HD**0.5
    tile = min(256, rows)
    tiles = group * rows // tile

    def absorb(block, key_base, first):
        def one(t, _):
            here = pl.ds(pl.multiple_of(t * tile, tile), tile)
            keys = kv[block, :, :, :HD].reshape(rows, HD)
            values = kv[block, :, :, HD:].reshape(rows, HD)
            score = lax.dot_general(
                query[here], keys, (((1,), (1,)), ((), ())), preferred_element_type=F32
            ) * scale
            key_pos = key_base + iota((1, rows), 1)
            if first:
                at = base + lax.rem(t * tile, rows) + iota((tile, 1), 0)
                allowed = (key_pos <= at) & (key_pos < length)
            else:
                allowed = key_pos < length
            score = jnp.where(allowed, score, -jnp.inf)
            old = jnp.full((tile, 1), -1e30, F32) if first else top[here]
            new = jnp.maximum(old, jnp.max(score, axis=-1, keepdims=True))
            weights = jnp.exp2(score - new)
            part = jnp.sum(weights, axis=-1, keepdims=True)
            out = dot(weights.astype(BF16), values)
            if first:
                total[here] = part
                acc[here] = out
            else:
                shrink = jnp.exp2(old - new)
                total[here] = total[here] * shrink + part
                acc[here] = acc[here] * shrink + out
            top[here] = new
            return 0

        lax.fori_loop(0, tiles, one, 0)

    absorb(core, base, True)

    @pl.when(core == 1)
    def _():
        for half in range(2):
            pair_copy(0, half, 0).wait_recv()
        absorb(0, base - rows, False)

    for hop in range(1, chips):
        @pl.when(chip >= hop)
        def _():
            for half in range(2):
                lane_copy(hop, half).wait_recv()
                if hop < chips - 1:
                    @pl.when(not_last)
                    def _():
                        lane_copy(hop + 1, half).start()
                pair_copy(hop, half, core).start()
            absorb(hop * 2 + core, base - 2 * hop * rows, False)
            for half in range(2):
                pair_copy(hop, half, other).wait_recv()
            absorb(hop * 2 + other, base - 2 * hop * rows + (other - core) * rows, False)

    for g in range(group):
        here = slice(g * rows, (g + 1) * rows)
        fine = base + iota((rows, 1), 0) < length
        attn = acc[here] / total[here]
        attn_ref[:, g * HD:(g + 1) * HD] = jnp.where(fine, attn, 0.0).astype(BF16)

    ring.drain()

    @pl.when(not_last)
    def _():
        for half in range(2):
            lane_copy(1, half).wait_send()

    @pl.when(core == 0)
    def _():
        for half in range(2):
            pair_copy(0, half, 0).wait_send()

    for hop in range(1, chips):
        @pl.when(chip >= hop)
        def _():
            for half in range(2):
                if hop < chips - 1:
                    @pl.when(not_last)
                    def _():
                        lane_copy(hop + 1, half).wait_send()
                pair_copy(hop, half, core).wait_send()


def mix_kernel(n_item, attn_ref, res_ref, wout_ref, out_ref, outgo, income, send, recv):
    me = lax.axis_index("item")
    rows = attn_ref.shape[0]
    half_rows = rows // 2
    cols = out_ref.shape[1]
    far = n_item // 2

    barrier = pltpu.get_barrier_semaphore()
    for step in (1, n_item - 1):
        signal(barrier, item=lax.rem(me + step, n_item))

    plan = []
    for way in range(2):
        steps = [(far, way)]
        for k in range(far - 1, 0, -1):
            steps += [(k, 1 - way), (k, way)]
        plan.append(steps)

    def partial(goal, half):
        here = pl.ds(pl.multiple_of(goal * cols, cols), cols)
        return dot(attn_ref[half * half_rows:(half + 1) * half_rows], wout_ref[:, here])

    def copy(way, at):
        step = 1 if way == 0 else n_item - 1
        return remote(
            outgo.at[way, at], income.at[way, at], send.at[way, at], recv.at[way, at],
            item=lax.rem(me + step, n_item),
        )

    for at in range(len(plan[0])):
        for way in range(2):
            k, half = plan[way][at]
            goal = lax.rem(me + (k if way == 0 else n_item - k), n_item)
            value = partial(goal, half)
            if (k + 1, half) in plan[way]:
                before = plan[way].index((k + 1, half))
                copy(way, before).wait_recv()
                value = value + income[way, before].astype(F32)
            outgo[way, at] = value.astype(BF16)
            if at == 0 and way == 0:
                pl.semaphore_wait(barrier, 2)
            copy(way, at).start()

    for half in (1, 0):
        here = slice(half * half_rows, (half + 1) * half_rows)
        value = partial(me, half) + res_ref[here].astype(F32)
        for way in range(2):
            if (1, half) in plan[way]:
                at = plan[way].index((1, half))
                copy(way, at).wait_recv()
                value = value + income[way, at].astype(F32)
        out_ref[here] = value.astype(BF16)
    for way in range(2):
        for at in range(len(plan[0])):
            copy(way, at).wait_send()


def vmem(count):
    return [pl.BlockSpec(memory_space=pltpu.VMEM)] * count


def params(number):
    return pltpu.CompilerParams(
        collective_id=number, has_side_effects=True, vmem_limit_bytes=VMEM_LIMIT
    )


def body(ny, item_states, item_gain, hist_ids, lengths, attn_gain, w_q, w_kv, q_gain, k_gain, w_out):
    n_seq = lax.axis_size("seq")
    n_item = lax.axis_size("item")
    nq = n_seq // ny
    per_dev, width = item_states.shape
    rows = hist_ids.shape[0]
    share = rows // n_item
    far = n_item // 2
    span = LEN // rows
    chips = span // CORES
    cols = width // n_item
    parts = 2
    dma = pltpu.SemaphoreType.DMA
    ids_row, ids_col = hist_ids.reshape(1, rows), hist_ids.reshape(rows, 1)

    fetched = pl.pallas_call(
        functools.partial(fetch_kernel, n_item, n_seq, ny),
        out_shape=jax.ShapeDtypeStruct((share, width), BF16),
        in_specs=vmem(4),
        out_specs=pl.BlockSpec(memory_space=pltpu.VMEM),
        scratch_shapes=[
            pltpu.VMEM((n_item * 2, per_dev // 2, width), BF16),
            pltpu.VMEM((ny, nq, 128), I32),
            pltpu.VMEM((ny, nq, 128), I32),
            pltpu.VMEM((nq, ny, 128), I32),
            pltpu.VMEM((nq, ny, 128), I32),
            pltpu.VMEM((parts, nq, 2 * ny, width // parts), BF16),
            pltpu.VMEM((parts, nq, 2 * ny, width // parts), BF16),
            pltpu.VMEM((parts, ny, 2 * nq, width // parts), BF16),
            pltpu.VMEM((parts, ny, 2 * nq, width // parts), BF16),
            dma((2, far, 2)), dma((2, far, 2)),
            dma((ny,)), dma((ny,)), dma((nq,)), dma((nq,)),
            dma((parts, nq)), dma((parts, nq)), dma((parts, ny)), dma((parts, ny)),
        ],
        compiler_params=params(1),
        name="fetch",
    )(ids_row, ids_col, item_states, item_gain.reshape(1, width))

    q_cols = w_q.shape[1]
    group = q_cols // HD
    attn, res = pl.pallas_call(
        functools.partial(attend_kernel, n_item, n_seq, per_dev),
        out_shape=[
            jax.ShapeDtypeStruct((rows, q_cols), BF16),
            jax.ShapeDtypeStruct((rows, cols), BF16),
        ],
        in_specs=vmem(2) + [pl.BlockSpec(memory_space=pltpu.SMEM)] + vmem(6),
        out_specs=vmem(2),
        scratch_shapes=[
            pltpu.VMEM((n_item * 2, share // 2, width), BF16),
            pltpu.VMEM((rows, q_cols + 2 * HD + cols), BF16),
            pltpu.VMEM((group * rows, HD), BF16),
            pltpu.VMEM((span, 2, rows // 2, 2 * HD), BF16),
            pltpu.VMEM((group * rows, HD), F32),
            pltpu.VMEM((group * rows, 1), F32),
            pltpu.VMEM((group * rows, 1), F32),
            dma((2, far, 2)), dma((2, far, 2)),
            dma((chips - 1, 2)), dma((chips - 1, 2)), dma((chips, 2)), dma((chips, 2)),
        ],
        compiler_params=params(2),
        name="attend",
    )(
        ids_row, ids_col, lengths, fetched, attn_gain.reshape(1, width), w_q,
        w_kv.reshape(width, 2 * HD), q_gain.reshape(1, HD), k_gain.reshape(1, HD),
    )

    steps = 2 * far - 1
    return pl.pallas_call(
        functools.partial(mix_kernel, n_item),
        out_shape=jax.ShapeDtypeStruct((rows, cols), BF16),
        in_specs=vmem(3),
        out_specs=pl.BlockSpec(memory_space=pltpu.VMEM),
        scratch_shapes=[
            pltpu.VMEM((2, steps, rows // 2, cols), BF16),
            pltpu.VMEM((2, steps, rows // 2, cols), BF16),
            dma((2, steps)), dma((2, steps)),
        ],
        compiler_params=params(3),
        name="mix",
    )(attn, res, w_out)


def solution(mesh):
    placed = (
        P(("item", "seq"), None),
        P(),
        P("seq"),
        P(),
        P(),
        P(None, "item"),
        P(None, None, "item"),
        P(),
        P(),
        P("item", None),
    )
    return jax.shard_map(
        functools.partial(body, NY),
        mesh=mesh, in_specs=placed, out_specs=P("seq", "item"), check_vma=False,
    )
```

```python
import functools

import jax
import jax.numpy as jnp
from jax import lax
from jax.experimental import pallas as pl
from jax.experimental.pallas import tpu as pltpu
from jax.sharding import PartitionSpec as P

HD = 128
LEN = 4096
CORES = 2
PARTS = 4
NY = 8
F32, BF16, I32 = jnp.float32, jnp.bfloat16, jnp.int32
VMEM_LIMIT = 48 * 1024 * 1024


def rms(x, gain):
    return x * lax.rsqrt(jnp.mean(x * x, axis=-1, keepdims=True) + 1e-06) * gain


def iota(shape, dim):
    return lax.broadcasted_iota(I32, shape, dim)


def onehot(mask):
    return jnp.where(mask, 1.0, 0.0).astype(BF16)


def dot(a, b):
    return jnp.dot(a, b, preferred_element_type=F32)


def signal(sem, **where):
    pl.semaphore_signal(sem, inc=1, device_id=where, device_id_type=pl.DeviceIdType.MESH)


def remote(src, dst, send, recv, **where):
    return pltpu.make_async_remote_copy(
        src_ref=src, dst_ref=dst, send_sem=send, recv_sem=recv,
        device_id=where, device_id_type=pl.DeviceIdType.MESH,
    )


class ZRing:
    def __init__(self, piece, send, recv, n):
        self.piece, self.send, self.recv, self.n = piece, send, recv, n
        self.far = n // 2
        self.me = lax.axis_index("item")

    def copy(self, way, part, hop, shard):
        step = 1 if way == 0 else self.n - 1
        ref = self.piece(part, shard, way if hop == self.far else None)
        at = (way, part, hop - 1)
        return remote(
            ref, ref, self.send.at[at], self.recv.at[at], item=lax.rem(self.me + step, self.n)
        )

    def shard(self, way, hop):
        return lax.rem(self.me + (self.n - hop if way == 0 else hop), self.n)

    def start(self, part):
        for way in range(2):
            self.copy(way, part, 1, self.me).start()

    def land(self, part, hop):
        for way in range(2):
            self.copy(way, part, hop, self.shard(way, hop)).wait_recv()
            if hop < self.far:
                self.copy(way, part, hop + 1, self.shard(way, hop)).start()

    def drain(self, parts):
        for part in range(parts):
            for hop in range(1, self.far + 1):
                for way in range(2):
                    self.copy(way, part, hop, self.shard(way, hop - 1)).wait_send()


def rank_of(ids_row, ids_col, per_dev, n_seq, axis):
    rows = ids_row.shape[1]
    owner_row = (ids_row // per_dev) & (n_seq - 1)
    owner_col = (ids_col // per_dev) & (n_seq - 1)
    lane, sub = iota((rows, rows), 1), iota((rows, rows), 0)
    if axis == 0:
        same = (owner_col == owner_row) & (sub < lane)
        less = owner_col < owner_row
    else:
        same = (owner_col == owner_row) & (lane < sub)
        less = owner_row < owner_col
    within = jnp.sum(jnp.where(same, 1.0, 0.0), axis=axis, keepdims=True).astype(I32)
    before = jnp.sum(jnp.where(less, 1.0, 0.0), axis=axis, keepdims=True).astype(I32)
    return before + within, within


def kernel(
    n_item, n_seq, ny, ids_row_ref, ids_col_ref, len_ref, states_ref, igain_ref, again_ref,
    qg_ref, kg_ref, wq_hbm, wkv_hbm, wout_hbm, out_ref,
    wq_ref, wkv_ref, wout_ref, table, id_a, id_b, id_c, id_d, found, mid, turned, final,
    every, sums, squares, mine, order, query, kv, bias, acc, top, total, attn_ref, res_ref, outgo, income,
    w_sem, t_send, t_recv, iy_send, iy_recv, ix_send, ix_recv, rx_send, rx_recv, ry_send, ry_recv,
    z_send, z_recv, lane_send, lane_recv, pair_send, pair_recv, o_send, o_recv,
):
    nq = n_seq // ny
    far = n_item // 2
    me = lax.axis_index("item")
    my_seq = lax.axis_index("seq")
    core = lax.rem(my_seq, CORES)
    other = 1 - core
    sibling = my_seq + 1 - 2 * core
    my_y = lax.rem(my_seq // CORES, ny)
    my_x = my_seq // (CORES * ny)
    my_q = my_x * CORES + core
    per_dev, width = states_ref.shape
    rows = ids_row_ref.shape[1]
    share = rows // n_item
    span = LEN // rows
    chips = span // CORES
    chip = lax.rem(my_seq // CORES, chips)
    not_last = chip < chips - 1
    base = lax.rem(my_seq, span) * rows
    length = len_ref[my_seq // span]
    q_cols = wq_ref.shape[1]
    group = q_cols // HD
    out_cols = width // n_item
    parts = found.shape[0]
    cols = width // parts

    def along_y(y):
        return (my_x * ny + y) * CORES + core

    def along_q(q):
        return ((q // CORES) * ny + my_y) * CORES + lax.rem(q, CORES)

    def y_plus(d):
        return lax.rem(my_y + d, ny)

    def q_plus(d):
        return lax.rem(my_q + d, nq)

    barrier = pltpu.get_barrier_semaphore()
    for step in (1, n_item - 1):
        signal(barrier, item=lax.rem(me + step, n_item))
    for d in range(1, ny):
        signal(barrier, seq=along_y(y_plus(d)))
    for d in range(1, nq):
        signal(barrier, seq=along_q(q_plus(d)))

    weights = [
        pltpu.make_async_copy(wq_hbm, wq_ref, w_sem.at[0]),
        pltpu.make_async_copy(wkv_hbm, wkv_ref, w_sem.at[1]),
        pltpu.make_async_copy(wout_hbm, wout_ref, w_sem.at[2]),
    ]
    for copy in weights:
        copy.start()

    embed = rms(states_ref[...].astype(F32), igain_ref[...]).astype(BF16)
    table[pl.ds(me * 2, 2)] = embed.reshape(2, per_dev // 2, width)
    pl.semaphore_wait(barrier, 2 + (ny - 1) + (nq - 1))

    def table_piece(part, shard, half):
        return table.at[pl.ds(shard * 2, 2)] if half is None else table.at[shard * 2 + half]

    items_ring = ZRing(table_piece, t_send, t_recv, n_item)
    items_ring.start(0)

    ids_row, ids_col = ids_row_ref[...], ids_col_ref[...]
    rank, within = rank_of(ids_row, ids_col, per_dev, n_seq, 0)
    owner = ids_row // per_dev
    owner_seq = owner & (n_seq - 1)
    source_y = (owner_seq // CORES) & (ny - 1)
    source_q = (owner_seq // (CORES * ny)) * CORES + (owner_seq & (CORES - 1))
    item = (owner // n_seq) * per_dev + (ids_row & (per_dev - 1)) + 1
    asks = (rank & (n_item - 1)) == me
    copy_no = within // n_item
    place = jnp.where(asks, source_y * nq + source_q, -1)
    asked = []
    for sub in range(2):
        hit = (iota((ny * nq, rows), 0) == place) & (copy_no == sub)
        asked.append(jnp.sum(jnp.where(hit, item.astype(F32), 0.0), axis=1, keepdims=True).astype(I32))
    lanes = iota((ny * nq, 128), 1)
    id_a[...] = jnp.where(lanes == 0, asked[0], jnp.where(lanes == 1, asked[1], 0)).reshape(ny, nq, 128)

    def ids_y(d, y_from, y_to):
        return remote(
            id_a.at[y_to], id_b.at[y_from], iy_send.at[d - 1], iy_recv.at[d - 1], seq=along_y(y_to)
        )

    def ids_q(d, q_from, q_to):
        return remote(
            id_c.at[q_to], id_d.at[q_from], ix_send.at[d - 1], ix_recv.at[d - 1], seq=along_q(q_to)
        )

    for d in range(1, ny):
        ids_y(d, my_y, y_plus(d)).start()
    id_b[my_y] = id_a[my_y]

    spot = jnp.where(asks, rank // n_item, -1)
    pick_a = onehot(iota((share, rows), 0) == spot)
    pick_b = onehot(iota((ny * nq * 2, rows), 0) == jnp.where(asks, place * 2 + copy_no, -1))
    pick = lax.dot_general(pick_a, pick_b, (((1,), (1,)), ((), ())), preferred_element_type=F32).astype(BF16)
    to, frm = iota((ny * nq * 2, nq * 2 * ny), 0), iota((ny * nq * 2, nq * 2 * ny), 1)
    to_y, to_q, to_sub = to // (nq * 2), (to // 2) % nq, to % 2
    turn = onehot(frm == (to_q * 2 + to_sub) * ny + to_y)

    for d in range(1, ny):
        ids_y(d, y_plus(ny - d), my_y).wait_recv()
    for q in range(nq):
        id_c[q] = id_b[:, q, :]
    for d in range(1, nq):
        ids_q(d, my_q, q_plus(d)).start()
    id_d[my_q] = id_c[my_q]
    items_ring.land(0, 1)

    def landing(rank):
        apart = (rank - me + n_item) & (n_item - 1)
        place = jnp.where(apart == 0, 0, jnp.where(apart < far, 2 * apart, 2 * (n_item - apart) - 1))
        return place * share + rank // n_item

    goal_row = landing(rank)
    pos_col = jnp.sum(
        jnp.where(goal_row == iota((rows, rows), 0), iota((rows, rows), 1).astype(F32), 0.0), axis=1, keepdims=True
    ).astype(I32)
    rank_col, _ = rank_of(ids_row, ids_col, per_dev, n_seq, 1)
    placed = landing(rank_col) == iota((rows, rows), 1)
    order[...] = onehot(placed)
    pos_row = jnp.sum(jnp.where(placed, iota((rows, rows), 0).astype(F32), 0.0), axis=0, keepdims=True).astype(I32)
    bias[core] = jnp.broadcast_to(jnp.where(base + pos_row < length, 0.0, -jnp.inf), (8, rows))
    items_ring.land(0, 2) if far > 1 else None

    chunks = [slice(0, 3 * share if far > 1 else 2 * share)]
    for hop in range(2, far + 1):
        chunks.append(slice((2 * hop - 1) * share, min(2 * hop + 1, n_item) * share))
    n_chunks = len(chunks)

    def block(slot, c):
        if c < 0:
            return bias.at[slot]
        return kv.at[slot, pl.ds(chunks[c].start, chunks[c].stop - chunks[c].start)]

    def lane_copy(hop, c):
        return remote(
            block((hop - 1) * 2 + core, c), block(hop * 2 + core, c),
            lane_send.at[hop - 1, c + 1], lane_recv.at[hop - 1, c + 1], seq=my_seq + CORES,
        )

    def pair_copy(hop, c, lane):
        return remote(
            block(hop * 2 + lane, c), block(hop * 2 + lane, c),
            pair_send.at[hop, c + 1], pair_recv.at[hop, c + 1], seq=sibling,
        )

    def give(c):
        @pl.when(not_last)
        def _():
            lane_copy(1, c).start()

        @pl.when(core == 0)
        def _():
            pair_copy(0, c, 0).start()

    def pass_on(stage):
        for hop in range(1, chips):
            c = stage - hop
            if -1 <= c < n_chunks:
                @pl.when(chip >= hop)
                def _():
                    lane_copy(hop, c).wait_recv()
                    if hop < chips - 1:
                        @pl.when(not_last)
                        def _():
                            lane_copy(hop + 1, c).start()
                    pair_copy(hop, c, core).start()

    give(-1)
    for hop in range(3, far + 1):
        items_ring.land(0, hop)

    for d in range(1, nq):
        ids_q(d, q_plus(nq - d), my_q).wait_recv()
    wanted = id_d[...].reshape(nq * ny, 128)
    names = iota((nq * ny, n_item * per_dev), 1) + 1
    choose = jnp.stack(
        [jnp.where(wanted[:, sub:sub + 1] == names, 1.0, 0.0).reshape(nq, ny, n_item * per_dev) for sub in range(2)],
        axis=1,
    ).reshape(nq * 2 * ny, n_item * per_dev).astype(BF16)

    def rows_q(part, d, q_from, q_to):
        return remote(
            found.at[part, q_to], mid.at[part, q_from],
            rx_send.at[part, d - 1], rx_recv.at[part, d - 1], seq=along_q(q_to),
        )

    def rows_y(part, d, y_from, y_to):
        return remote(
            turned.at[part, y_to], final.at[part, y_from],
            ry_send.at[part, d - 1], ry_recv.at[part, d - 1], seq=along_y(y_to),
        )

    for part in range(parts):
        source = table[:, :, part * cols:(part + 1) * cols].reshape(n_item * per_dev, cols)
        found[part] = dot(choose, source).astype(BF16).reshape(nq, 2 * ny, cols)
        for d in range(1, nq):
            rows_q(part, d, my_q, q_plus(d)).start()
        mid[part, my_q] = found[part, my_q]
    for part in range(parts):
        for d in range(1, nq):
            rows_q(part, d, q_plus(nq - d), my_q).wait_recv()
        turned[part] = dot(turn, mid[part].reshape(nq * 2 * ny, cols)).astype(BF16).reshape(ny, 2 * nq, cols)
        for d in range(1, ny):
            rows_y(part, d, my_y, y_plus(d)).start()
        final[part, my_y] = turned[part, my_y]

    def rows_piece(part, shard, half):
        return every.at[part, pl.ds(shard * 2, 2)] if half is None else every.at[part, shard * 2 + half]

    ring = ZRing(rows_piece, z_send, z_recv, n_item)

    def arrive(part):
        for d in range(1, ny):
            rows_y(part, d, y_plus(ny - d), my_y).wait_recv()
        got = dot(pick, final[part].reshape(ny * 2 * nq, cols)).astype(BF16)
        every[part, pl.ds(me * 2, 2)] = got.reshape(2, share // 2, cols)
        ring.start(part)

    def project(part, hop):
        shards = [me] if hop == 0 else [ring.shard(0, hop)] + ([ring.shard(1, hop)] if hop < far else [])
        first = 0 if hop == 0 else (2 * hop - 1) * share
        here = slice(first, first + len(shards) * share)
        x = jnp.concatenate([every[part, pl.ds(j * 2, 2)].reshape(share, cols) for j in shards], axis=0).astype(F32)
        span = slice(part * cols, (part + 1) * cols)
        y = (x * again_ref[:, span]).astype(BF16)
        q = dot(y, wq_ref[span])
        pair = dot(y, wkv_ref[span])
        square = jnp.sum(x * x, axis=-1, keepdims=True)
        if part > 0:
            q = q + sums[here, :q_cols]
            pair = pair + sums[here, q_cols:]
            square = square + squares[here]
        if part < parts - 1:
            sums[here, :q_cols] = q
            sums[here, q_cols:] = pair
            squares[here] = square
            return
        scale = lax.rsqrt(square / width + 1e-06)
        q, pair = q * scale, pair * scale
        for g in range(group):
            query[g * rows + here.start:g * rows + here.stop] = rms(q[:, g * HD:(g + 1) * HD], qg_ref[...]).astype(BF16)
        kv[core, here, :HD] = rms(pair[:, :HD], kg_ref[...]).astype(BF16)
        kv[core, here, HD:] = pair[:, HD:].astype(BF16)

    def projected(part, hop):
        project(part, hop)
        if part == parts - 1 and hop > 0:
            give(hop - 1)
            pass_on(hop - 1)

    for diagonal in range(parts + far):
        now = [(part, diagonal - part) for part in range(parts) if 1 <= diagonal - part <= far]
        for part, hop in now:
            ring.land(part, hop)
        if diagonal < parts:
            arrive(diagonal)
        if diagonal == 0:
            for copy in weights:
                copy.wait()
        for part, hop in now:
            projected(part, hop)
        if diagonal < parts:
            projected(diagonal, 0)

    scale = 1.4426950408889634 / HD**0.5

    def absorb(blocks, first):
        for g in range(group):
            here = slice(g * rows, (g + 1) * rows)
            q = query[here]
            if first:
                old = jnp.full((rows, 1), -1e30, F32)
            else:
                old, whole, out = top[here], total[here], acc[here]
            for slot in blocks:
                score = lax.dot_general(
                    q, kv[slot, :, :HD], (((1,), (1,)), ((), ())), preferred_element_type=F32
                ) * scale + bias[slot, 0:1]
                if first:
                    score = jnp.where(pos_row <= pos_col, score, -jnp.inf)
                new = jnp.maximum(old, jnp.max(score, axis=-1, keepdims=True))
                weights = jnp.exp2(score - new)
                part = jnp.sum(weights, axis=-1, keepdims=True)
                more = dot(weights.astype(BF16), kv[slot, :, HD:])
                if first:
                    whole, out = part, more
                else:
                    shrink = jnp.exp2(old - new)
                    whole, out = whole * shrink + part, out * shrink + more
                old = new
            top[here], total[here], acc[here] = old, whole, out

    stage = far
    absorb([core], True)
    pass_on(stage)

    @pl.when(core == 1)
    def _():
        for c in range(-1, n_chunks):
            pair_copy(0, c, 0).wait_recv()
        absorb([0], False)

    for hop in range(1, chips):
        stage += 1
        pass_on(stage)

        @pl.when(chip >= hop)
        def _():
            for c in range(-1, n_chunks):
                pair_copy(hop, c, other).wait_recv()
            absorb([hop * 2 + core, hop * 2 + other], False)

    seen = jnp.concatenate(
        [(acc[g * rows:(g + 1) * rows] / total[g * rows:(g + 1) * rows]).astype(BF16) for g in range(group)], axis=1
    )
    fine = base + iota((rows, 1), 0) < length
    attn_ref[...] = jnp.where(fine, dot(order[...], seen), 0.0).astype(BF16)

    half_rows = rows // 2
    plan = []
    for way in range(2):
        steps = [(far, way)]
        for k in range(far - 1, 0, -1):
            steps += [(k, 1 - way), (k, way)]
        plan.append(steps)

    def partial(goal, half):
        here = pl.ds(pl.multiple_of(goal * out_cols, out_cols), out_cols)
        return dot(attn_ref[half * half_rows:(half + 1) * half_rows], wout_ref[:, here])

    def sum_copy(way, at):
        step = 1 if way == 0 else n_item - 1
        return remote(
            outgo.at[way, at], income.at[way, at], o_send.at[way, at], o_recv.at[way, at],
            item=lax.rem(me + step, n_item),
        )

    for at in range(len(plan[0])):
        for way in range(2):
            k, half = plan[way][at]
            goal = lax.rem(me + (k if way == 0 else n_item - k), n_item)
            value = partial(goal, half)
            if (k + 1, half) in plan[way]:
                before = plan[way].index((k + 1, half))
                sum_copy(way, before).wait_recv()
                value = value + income[way, before].astype(F32)
            outgo[way, at] = value.astype(BF16)
            sum_copy(way, at).start()
        if at == min(1, len(plan[0]) - 1):
            where = me * out_cols
            inside = pl.ds(pl.multiple_of(lax.rem(where, cols), out_cols), out_cols)
            for hop in range(far + 1):
                for way in range(2 if 0 < hop < far else 1):
                    j = ring.shard(way, hop) if hop > 0 else me
                    first = 0 if hop == 0 else (2 * hop - 1 + way) * share
                    mine[first:first + share] = every[where // cols, pl.ds(j * 2, 2), :, inside].reshape(share, out_cols)
            res_ref[...] = dot(order[...], mine[...]).astype(BF16)

    for half in (1, 0):
        here = slice(half * half_rows, (half + 1) * half_rows)
        value = partial(me, half) + res_ref[here].astype(F32)
        for way in range(2):
            if (1, half) in plan[way]:
                at = plan[way].index((1, half))
                sum_copy(way, at).wait_recv()
                value = value + income[way, at].astype(F32)
        out_ref[here] = value.astype(BF16)

    items_ring.drain(1)
    ring.drain(parts)
    for d in range(1, ny):
        ids_y(d, my_y, y_plus(d)).wait_send()
    for d in range(1, nq):
        ids_q(d, my_q, q_plus(d)).wait_send()
    for part in range(parts):
        for d in range(1, nq):
            rows_q(part, d, my_q, q_plus(d)).wait_send()
        for d in range(1, ny):
            rows_y(part, d, my_y, y_plus(d)).wait_send()
    for c in range(-1, n_chunks):
        @pl.when(not_last)
        def _():
            lane_copy(1, c).wait_send()

        @pl.when(core == 0)
        def _():
            pair_copy(0, c, 0).wait_send()

        for hop in range(1, chips):
            @pl.when(chip >= hop)
            def _():
                if hop < chips - 1:
                    @pl.when(not_last)
                    def _():
                        lane_copy(hop + 1, c).wait_send()
                pair_copy(hop, c, core).wait_send()
    for way in range(2):
        for at in range(len(plan[0])):
            sum_copy(way, at).wait_send()


def body(ny, item_states, item_gain, hist_ids, lengths, attn_gain, w_q, w_kv, q_gain, k_gain, w_out):
    n_seq = lax.axis_size("seq")
    n_item = lax.axis_size("item")
    nq = n_seq // ny
    per_dev, width = item_states.shape
    rows = hist_ids.shape[0]
    share = rows // n_item
    far = n_item // 2
    span = LEN // rows
    chips = span // CORES
    out_cols = width // n_item
    q_cols = w_q.shape[1]
    group = q_cols // HD
    cols = width // PARTS
    steps = 2 * far - 1
    dma = pltpu.SemaphoreType.DMA
    vmem, smem, hbm = (pl.BlockSpec(memory_space=space) for space in (pltpu.VMEM, pltpu.SMEM, pl.ANY))
    return pl.pallas_call(
        functools.partial(kernel, n_item, n_seq, ny),
        out_shape=jax.ShapeDtypeStruct((rows, out_cols), BF16),
        in_specs=[vmem] * 2 + [smem] + [vmem] * 5 + [hbm] * 3,
        out_specs=vmem,
        scratch_shapes=[
            pltpu.VMEM((width, q_cols), BF16),
            pltpu.VMEM((width, 2 * HD), BF16),
            pltpu.VMEM((q_cols, width), BF16),
            pltpu.VMEM((n_item * 2, per_dev // 2, width), BF16),
            pltpu.VMEM((ny, nq, 128), I32),
            pltpu.VMEM((ny, nq, 128), I32),
            pltpu.VMEM((nq, ny, 128), I32),
            pltpu.VMEM((nq, ny, 128), I32),
            pltpu.VMEM((PARTS, nq, 2 * ny, cols), BF16),
            pltpu.VMEM((PARTS, nq, 2 * ny, cols), BF16),
            pltpu.VMEM((PARTS, ny, 2 * nq, cols), BF16),
            pltpu.VMEM((PARTS, ny, 2 * nq, cols), BF16),
            pltpu.VMEM((PARTS, n_item * 2, share // 2, cols), BF16),
            pltpu.VMEM((rows, q_cols + 2 * HD), F32),
            pltpu.VMEM((rows, 1), F32),
            pltpu.VMEM((rows, out_cols), BF16),
            pltpu.VMEM((rows, rows), BF16),
            pltpu.VMEM((group * rows, HD), BF16),
            pltpu.VMEM((span, rows, 2 * HD), BF16),
            pltpu.VMEM((span, 8, rows), F32),
            pltpu.VMEM((group * rows, HD), F32),
            pltpu.VMEM((group * rows, 1), F32),
            pltpu.VMEM((group * rows, 1), F32),
            pltpu.VMEM((rows, q_cols), BF16),
            pltpu.VMEM((rows, out_cols), BF16),
            pltpu.VMEM((2, steps, rows // 2, out_cols), BF16),
            pltpu.VMEM((2, steps, rows // 2, out_cols), BF16),
            dma((3,)),
            dma((2, 1, far)), dma((2, 1, far)),
            dma((ny,)), dma((ny,)), dma((nq,)), dma((nq,)),
            dma((PARTS, nq)), dma((PARTS, nq)), dma((PARTS, ny)), dma((PARTS, ny)),
            dma((2, PARTS, far)), dma((2, PARTS, far)),
            dma((chips - 1, far + 1)), dma((chips - 1, far + 1)),
            dma((chips, far + 1)), dma((chips, far + 1)),
            dma((2, steps)), dma((2, steps)),
        ],
        compiler_params=pltpu.CompilerParams(
            collective_id=1, has_side_effects=True, vmem_limit_bytes=VMEM_LIMIT
        ),
        name="user_layer",
    )(
        hist_ids.reshape(1, rows), hist_ids.reshape(rows, 1), lengths, item_states,
        item_gain.reshape(1, width), attn_gain.reshape(1, width), q_gain.reshape(1, HD),
        k_gain.reshape(1, HD), w_q, w_kv.reshape(width, 2 * HD), w_out,
    )


def solution(mesh):
    placed = (
        P(("item", "seq"), None),
        P(),
        P("seq"),
        P(),
        P(),
        P(None, "item"),
        P(None, None, "item"),
        P(),
        P(),
        P("item", None),
    )
    return jax.shard_map(
        functools.partial(body, NY),
        mesh=mesh, in_specs=placed, out_specs=P("seq", "item"), check_vma=False,
    )
```

```python
import functools

import jax
import jax.numpy as jnp
from jax import lax
from jax.experimental import pallas as pl
from jax.experimental.pallas import tpu as pltpu
from jax.sharding import PartitionSpec as P

HD = 128
LEN = 4096
CORES = 2
PARTS = 2
NY = 8
F32, BF16, I32 = jnp.float32, jnp.bfloat16, jnp.int32
VMEM_LIMIT = 61 * 1024 * 1024


def rms(x, gain):
    return x * lax.rsqrt(jnp.mean(x * x, axis=-1, keepdims=True) + 1e-06) * gain


def iota(shape, dim):
    return lax.broadcasted_iota(I32, shape, dim)


def onehot(mask):
    return jnp.where(mask, 1.0, 0.0).astype(BF16)


def dot(a, b):
    return jnp.dot(a, b, preferred_element_type=F32)


def signal(sem, **where):
    pl.semaphore_signal(sem, inc=1, device_id=where, device_id_type=pl.DeviceIdType.MESH)


def remote(src, dst, send, recv, **where):
    return pltpu.make_async_remote_copy(
        src_ref=src, dst_ref=dst, send_sem=send, recv_sem=recv,
        device_id=where, device_id_type=pl.DeviceIdType.MESH,
    )


class ZRing:
    def __init__(self, piece, send, recv, n):
        self.piece, self.send, self.recv, self.n = piece, send, recv, n
        self.far = n // 2
        self.me = lax.axis_index("item")

    def copy(self, way, part, hop, shard):
        step = 1 if way == 0 else self.n - 1
        ref = self.piece(part, shard, way if hop == self.far else None)
        at = (way, part, hop - 1)
        return remote(
            ref, ref, self.send.at[at], self.recv.at[at], item=lax.rem(self.me + step, self.n)
        )

    def shard(self, way, hop):
        return lax.rem(self.me + (self.n - hop if way == 0 else hop), self.n)

    def start(self, part):
        for way in range(2):
            self.copy(way, part, 1, self.me).start()

    def land(self, part, hop):
        for way in range(2):
            self.copy(way, part, hop, self.shard(way, hop)).wait_recv()
            if hop < self.far:
                self.copy(way, part, hop + 1, self.shard(way, hop)).start()

    def drain(self, parts):
        for part in range(parts):
            for hop in range(1, self.far + 1):
                for way in range(2):
                    self.copy(way, part, hop, self.shard(way, hop - 1)).wait_send()


def rank_of(ids_row, ids_col, per_dev, n_seq, axis):
    rows = ids_row.shape[1]
    owner_row = (ids_row // per_dev) & (n_seq - 1)
    owner_col = (ids_col // per_dev) & (n_seq - 1)
    lane, sub = iota((rows, rows), 1), iota((rows, rows), 0)
    if axis == 0:
        same = (owner_col == owner_row) & (sub < lane)
        less = owner_col < owner_row
    else:
        same = (owner_col == owner_row) & (lane < sub)
        less = owner_row < owner_col
    within = jnp.sum(jnp.where(same, 1.0, 0.0), axis=axis, keepdims=True).astype(I32)
    before = jnp.sum(jnp.where(less, 1.0, 0.0), axis=axis, keepdims=True).astype(I32)
    return before + within, within


def kernel(
    n_item, n_seq, ny, len_ref, ids_hbm, states_hbm, igain_hbm, again_hbm, qg_hbm, kg_hbm,
    wq_hbm, wkv_hbm, wout_hbm, out_ref, ids_row_ref, states_ref, igain_ref, again_ref, qg_ref, kg_ref,
    wq_ref, wkv_raw, wkv_ref, wout_ref, table, id_a, id_b, id_c, id_d, wide, parcel, landed,
    every, order, query, kv, bias, acc, top, total, attn_ref, res_ref, outgo, income,
    w_sem, t_send, t_recv, iy_send, iy_recv, ix_send, ix_recv, row_send, row_recv,
    z_send, z_recv, lane_send, lane_recv, pair_send, pair_recv, o_send, o_recv,
):
    nq = n_seq // ny
    far = n_item // 2
    me = lax.axis_index("item")
    my_seq = lax.axis_index("seq")
    core = lax.rem(my_seq, CORES)
    other = 1 - core
    sibling = my_seq + 1 - 2 * core
    my_y = lax.rem(my_seq // CORES, ny)
    my_x = my_seq // (CORES * ny)
    my_q = my_x * CORES + core
    per_dev, width = states_ref.shape
    rows = ids_row_ref.shape[1]
    share = rows // n_item
    span = LEN // rows
    chips = span // CORES
    chip = lax.rem(my_seq // CORES, chips)
    not_last = chip < chips - 1
    base = lax.rem(my_seq, span) * rows
    length = len_ref[my_seq // span]
    q_cols = wq_ref.shape[1]
    group = q_cols // HD
    out_cols = width // n_item
    parts = every.shape[0]
    cols = width // parts

    def along_y(y):
        return (my_x * ny + y) * CORES + core

    def along_q(q):
        return ((q // CORES) * ny + my_y) * CORES + lax.rem(q, CORES)

    def y_plus(d):
        return lax.rem(my_y + d, ny)

    def q_plus(d):
        return lax.rem(my_q + d, nq)

    n_mate = nq * ny
    my_mate = my_q * ny + my_y

    def mate_seq(m):
        q, y = m // ny, lax.rem(m, ny)
        return ((q // CORES) * ny + y) * CORES + lax.rem(q, CORES)

    def to_mates(do):
        def one(d, _):
            do(lax.rem(my_mate + d, n_mate))
            do(lax.rem(my_mate + n_mate - d, n_mate))
            return 0

        lax.fori_loop(1, n_mate // 2, one, 0)
        do(lax.rem(my_mate + n_mate // 2, n_mate))

    barrier = pltpu.get_barrier_semaphore()
    for step in (1, n_item - 1):
        signal(barrier, item=lax.rem(me + step, n_item))
    to_mates(lambda m: signal(barrier, seq=mate_seq(m)))

    small = [(states_hbm, states_ref), (igain_hbm, igain_ref), (ids_hbm, ids_row_ref)]
    large = [(again_hbm, again_ref), (qg_hbm, qg_ref), (kg_hbm, kg_ref)]
    large += [(wq_hbm, wq_ref), (wkv_hbm, wkv_raw), (wout_hbm, wout_ref)]
    small, large = (
        [pltpu.make_async_copy(a, b, w_sem.at[at + i]) for i, (a, b) in enumerate(pairs)]
        for at, pairs in ((0, small), (len(small), large))
    )
    for copy in small + large:
        copy.start()
    for copy in small:
        copy.wait()

    embed = rms(states_ref[...].astype(F32), igain_ref[...]).astype(BF16)
    for part in range(parts):
        table[part, me] = embed[:, part * cols:(part + 1) * cols]
    pl.semaphore_wait(barrier, 2 + n_mate - 1)

    def table_piece(part, shard, way):
        if way is None:
            return table.at[part, shard]
        return table.at[part, shard, pl.ds(way * (per_dev // 2), per_dev // 2)]

    items_ring = ZRing(table_piece, t_send, t_recv, n_item)
    for part in range(parts):
        items_ring.start(part)

    def land_items(hop):
        for part in range(parts):
            items_ring.land(part, hop)

    ids_row = ids_row_ref[...]
    diagonal = iota((rows, rows), 0) == iota((rows, rows), 1)
    ids_col = jnp.sum(jnp.where(diagonal, ids_row.astype(F32), 0.0), axis=1, keepdims=True).astype(I32)
    rank, within = rank_of(ids_row, ids_col, per_dev, n_seq, 0)
    owner = ids_row // per_dev
    owner_seq = owner & (n_seq - 1)
    source_y = (owner_seq // CORES) & (ny - 1)
    source_q = (owner_seq // (CORES * ny)) * CORES + (owner_seq & (CORES - 1))
    item = (owner // n_seq) * per_dev + (ids_row & (per_dev - 1)) + 1
    asks_at = rank & (n_item - 1)
    asks = asks_at == me
    copy_no = within // n_item
    place = jnp.where(asks, source_y * nq + source_q, -1)
    asked = []
    for sub in range(2):
        hit = (iota((ny * nq, rows), 0) == place) & (copy_no == sub)
        asked.append(jnp.sum(jnp.where(hit, item.astype(F32), 0.0), axis=1, keepdims=True).astype(I32))
    lanes = iota((ny * nq, 128), 1)
    id_a[...] = jnp.where(lanes == 0, asked[0], jnp.where(lanes == 1, asked[1], 0)).reshape(ny, nq, 128)

    def ids_y(d, y_from, y_to):
        return remote(
            id_a.at[y_to], id_b.at[y_from], iy_send.at[d - 1], iy_recv.at[d - 1], seq=along_y(y_to)
        )

    def ids_q(d, q_from, q_to):
        return remote(
            id_c.at[q_to], id_d.at[q_from], ix_send.at[d - 1], ix_recv.at[d - 1], seq=along_q(q_to)
        )

    for d in range(1, ny):
        ids_y(d, my_y, y_plus(d)).start()
    id_b[my_y] = id_a[my_y]

    spot = jnp.where(asks, rank // n_item, -1)
    pick_a = onehot(iota((share, rows), 0) == spot)
    sent = jnp.where(asks, copy_no * n_mate + source_q * ny + source_y, -1)
    pick_b = onehot(iota((2 * n_mate, rows), 0) == sent)
    pick = lax.dot_general(pick_a, pick_b, (((1,), (1,)), ((), ())), preferred_element_type=F32).astype(BF16)

    for d in range(1, ny):
        ids_y(d, y_plus(ny - d), my_y).wait_recv()
    for q in range(nq):
        id_c[q] = id_b[:, q, :]
    for d in range(1, nq):
        ids_q(d, my_q, q_plus(d)).start()
    id_d[my_q] = id_c[my_q]
    land_items(1)

    def landing(rank):
        apart = (rank - me + n_item) & (n_item - 1)
        place = jnp.where(apart == 0, 0, jnp.where(apart < far, 2 * apart, 2 * (n_item - apart) - 1))
        return place * share + rank // n_item

    goal_row = asks_at * share + rank // n_item
    pos_col = jnp.sum(
        jnp.where(goal_row == iota((rows, rows), 0), iota((rows, rows), 1).astype(F32), 0.0), axis=1, keepdims=True
    ).astype(I32)
    rank_col, _ = rank_of(ids_row, ids_col, per_dev, n_seq, 1)
    order[...] = onehot((rank_col & (n_item - 1)) * share + rank_col // n_item == iota((rows, rows), 1))
    placed = landing(rank_col) == iota((rows, rows), 1)
    pos_row = jnp.sum(jnp.where(placed, iota((rows, rows), 0).astype(F32), 0.0), axis=0, keepdims=True).astype(I32)
    bias[core] = jnp.broadcast_to(jnp.where(base + pos_row < length, 0.0, -jnp.inf), (8, rows))
    if far > 2:
        land_items(2)

    chunks = [slice(0, 3 * share if far > 1 else 2 * share)]
    for hop in range(2, far + 1):
        chunks.append(slice((2 * hop - 1) * share, min(2 * hop + 1, n_item) * share))
    n_chunks = len(chunks)

    def block(slot, c):
        if c < 0:
            return bias.at[slot]
        return kv.at[slot, pl.ds(chunks[c].start, chunks[c].stop - chunks[c].start)]

    def lane_copy(hop, c, far_off=False):
        return remote(
            block(core if far_off else (hop - 1) * 2 + core, c), block(hop * 2 + core, c),
            lane_send.at[hop - 1, c + 1], lane_recv.at[hop - 1, c + 1],
            seq=my_seq + (hop if far_off else 1) * CORES,
        )

    def pair_copy(hop, c, lane):
        return remote(
            block(hop * 2 + lane, c), block(hop * 2 + lane, c),
            pair_send.at[hop, c + 1], pair_recv.at[hop, c + 1], seq=sibling,
        )

    straight = range(n_chunks - 1, n_chunks)

    def give(c):
        if c in straight:
            for hop in range(1, chips):
                @pl.when(chip + hop < chips)
                def _():
                    lane_copy(hop, c, True).start()
        else:
            @pl.when(not_last)
            def _():
                lane_copy(1, c).start()

        @pl.when(core == 0)
        def _():
            pair_copy(0, c, 0).start()

    def take(hop, c):
        @pl.when(chip >= hop)
        def _():
            lane_copy(hop, c).wait_recv()
            if hop < chips - 1 and c not in straight:
                @pl.when(not_last)
                def _():
                    lane_copy(hop + 1, c).start()
            pair_copy(hop, c, core).start()

    def pass_on(stage):
        for hop in range(1, chips):
            for c in range(-1, n_chunks):
                if c not in straight and 2 * (c + 1) + hop == stage:
                    take(hop, c)

    give(-1)
    for hop in range(3, far):
        land_items(hop)
    for copy in large:
        copy.wait()
    strip = min(128, width)
    to, frm = iota((2 * strip, 2 * strip), 0), iota((2 * strip, 2 * strip), 1)
    split = onehot(frm == lax.rem(to, strip) * 2 + to // strip)
    for first in range(0, width, strip):
        both = dot(split, wkv_raw[first * 2:(first + strip) * 2]).astype(BF16)
        wkv_ref[first:first + strip, :HD] = both[:strip]
        wkv_ref[first:first + strip, HD:] = both[strip:]

    for d in range(1, nq):
        ids_q(d, q_plus(nq - d), my_q).wait_recv()
    wanted = id_d[...].reshape(nq * ny, 128)
    names = iota((nq * ny, n_item * per_dev), 1) + 1
    choose = [onehot(wanted[:, sub:sub + 1] == names) for sub in range(2)]
    blocks = width // HD
    tall = 2 * blocks

    def rows_copy(m_from, m_to):
        return remote(
            parcel.at[m_to], landed.at[m_from], row_send.at[0], row_recv.at[0], seq=mate_seq(m_to)
        )

    def all_but_one(buf, sem):
        ref = buf.at[pl.ds(0, n_mate - 1)]
        return pltpu.make_async_copy(ref, ref, sem.at[0])

    def rows_piece(part, shard, way):
        if way is None:
            return every.at[part, shard]
        return every.at[part, shard, pl.ds(way * (share // 2), share // 2)]

    ring = ZRing(rows_piece, z_send, z_recv, n_item)

    for part in range(parts):
        if far > 1:
            items_ring.land(part, far)
        source = table[part].reshape(n_item * per_dev, cols)
        for sub in range(2):
            picked = dot(choose[sub], source)
            for k in range(cols // HD):
                at = sub * blocks + part * (cols // HD) + k
                wide[pl.ds(at, n_mate, stride=tall), :] = picked[:, k * HD:(k + 1) * HD]
    parcel[...] = wide[...].reshape(n_mate, tall, HD).astype(BF16)
    to_mates(lambda m: rows_copy(my_mate, m).start())
    landed[my_mate] = parcel[my_mate]

    all_but_one(landed, row_recv).wait()
    wide[...] = landed[...].reshape(n_mate * tall, HD).astype(F32)
    for part in range(parts):
        for k in range(cols // HD):
            at = part * (cols // HD) + k
            came = jnp.concatenate(
                [wide[pl.ds(sub * blocks + at, n_mate, stride=tall), :] for sub in range(2)], axis=0
            ).astype(BF16)
            every[part, me, :, k * HD:(k + 1) * HD] = dot(pick, came).astype(BF16)
        ring.start(part)

    scale = 1.4426950408889634 / HD**0.5

    def project(hop):
        shards = [me] if hop == 0 else [ring.shard(0, hop)] + ([ring.shard(1, hop)] if hop < far else [])
        first = 0 if hop == 0 else (2 * hop - 1) * share
        here = slice(first, first + len(shards) * share)
        x = jnp.concatenate(
            [jnp.concatenate([every[part, j] for part in range(parts)], axis=1) for j in shards], axis=0
        )
        normed = rms(x.astype(F32), again_ref[...]).astype(BF16)
        q = dot(normed, wq_ref[...])
        key = dot(normed, wkv_ref[:, :HD])
        value = dot(normed, wkv_ref[:, HD:])
        for g in range(group):
            piece = rms(q[:, g * HD:(g + 1) * HD], qg_ref[...] * scale).astype(BF16)
            for at, j in enumerate(shards):
                there = pl.ds(pl.multiple_of(g * rows + j * share, share), share)
                query[there] = piece[at * share:(at + 1) * share]
        kv[core, here, :HD] = rms(key, kg_ref[...]).astype(BF16)
        kv[core, here, HD:] = value.astype(BF16)

    project(0)
    for hop in range(1, far + 1):
        ring.land(0, hop)
        pass_on(2 * hop - 1)
        ring.land(1, hop)
        project(hop)
        give(hop - 1)
        pass_on(2 * hop)

    def spread(x):
        return x[:, :rows] if rows < HD else jnp.concatenate([x] * (rows // HD), axis=1)

    def absorb(blocks, first):
        for g in range(group):
            here = slice(g * rows, (g + 1) * rows)
            q = query[here]
            if first:
                old = jnp.full((rows, HD), -1e30, F32)
            else:
                old, whole, out = top[here], total[here], acc[here]
            for slot in blocks:
                score = lax.dot_general(
                    q, kv[slot, :, :HD], (((1,), (1,)), ((), ())), preferred_element_type=F32
                ) + bias[slot, 0:1]
                if first:
                    score = jnp.where(pos_row <= pos_col, score, -jnp.inf)
                new = jnp.maximum(old, jnp.max(score, axis=-1, keepdims=True))
                weights = jnp.exp2(score - spread(new))
                part = jnp.sum(weights, axis=-1, keepdims=True)
                more = dot(weights.astype(BF16), kv[slot, :, HD:])
                if first:
                    whole, out = jnp.broadcast_to(part, (rows, HD)), more
                else:
                    shrink = jnp.exp2(old - new)
                    whole, out = whole * shrink + part, out * shrink + more
                old = new
            top[here], total[here], acc[here] = old, whole, out

    absorb([core], True)
    pass_on(2 * far + 1)
    take(1, straight[0])

    @pl.when(core == 1)
    def _():
        for c in range(-1, n_chunks):
            pair_copy(0, c, 0).wait_recv()
        absorb([0], False)

    for stage in range(2 * far + 2, 2 * far + chips):
        pass_on(stage)
    for hop in range(2, chips):
        take(hop, straight[0])
    for last in range(1, chips):
        @pl.when(chip == last)
        def _():
            for hop in range(1, last + 1):
                for c in range(-1, n_chunks):
                    pair_copy(hop, c, other).wait_recv()
            absorb([2 * hop + lane for hop in range(1, last + 1) for lane in range(2)], False)

    seen = jnp.concatenate(
        [(acc[g * rows:(g + 1) * rows] / total[g * rows:(g + 1) * rows]).astype(BF16) for g in range(group)], axis=1
    )
    fine = base + pos_col < length
    attn_ref[...] = jnp.where(fine, seen, jnp.zeros_like(seen))

    half_rows = rows // 2
    plan = []
    for way in range(2):
        steps = [(far, way)]
        for k in range(far - 1, 0, -1):
            steps += [(k, 1 - way), (k, way)]
        plan.append(steps)

    def partial(goal, half):
        here = pl.ds(pl.multiple_of(goal * out_cols, out_cols), out_cols)
        return dot(attn_ref[half * half_rows:(half + 1) * half_rows], wout_ref[:, here])

    def sum_copy(way, at):
        step = 1 if way == 0 else n_item - 1
        return remote(
            outgo.at[way, at], income.at[way, at], o_send.at[way, at], o_recv.at[way, at],
            item=lax.rem(me + step, n_item),
        )

    for at in range(len(plan[0])):
        for way in range(2):
            k, half = plan[way][at]
            goal = lax.rem(me + (k if way == 0 else n_item - k), n_item)
            value = partial(goal, half)
            if (k + 1, half) in plan[way]:
                before = plan[way].index((k + 1, half))
                sum_copy(way, before).wait_recv()
                value = value + income[way, before].astype(F32)
            outgo[way, at] = value.astype(BF16)
            sum_copy(way, at).start()
    where = me * out_cols
    inside = pl.ds(pl.multiple_of(lax.rem(where, cols), out_cols), out_cols)
    for half in (1, 0):
        here = slice(half * half_rows, (half + 1) * half_rows)
        first = half * (n_item // 2)
        own = every[where // cols, first:first + n_item // 2, :, inside].reshape(half_rows, out_cols)
        value = partial(me, half) + own.astype(F32)
        for way in range(2):
            if (1, half) in plan[way]:
                at = plan[way].index((1, half))
                sum_copy(way, at).wait_recv()
                value = value + income[way, at].astype(F32)
        res_ref[here] = value.astype(BF16)
    out_ref[...] = dot(order[...], res_ref[...]).astype(BF16)

    items_ring.drain(parts)
    ring.drain(parts)
    for d in range(1, ny):
        ids_y(d, my_y, y_plus(d)).wait_send()
    for d in range(1, nq):
        ids_q(d, my_q, q_plus(d)).wait_send()
    all_but_one(parcel, row_send).wait()
    for c in range(-1, n_chunks):
        @pl.when(core == 0)
        def _():
            pair_copy(0, c, 0).wait_send()

        for hop in range(1, chips):
            if c in straight:
                @pl.when(chip + hop < chips)
                def _():
                    lane_copy(hop, c, True).wait_send()
            else:
                @pl.when((chip >= hop - 1) & not_last)
                def _():
                    lane_copy(hop, c).wait_send()

            @pl.when(chip >= hop)
            def _():
                pair_copy(hop, c, core).wait_send()

    for way in range(2):
        for at in range(len(plan[0])):
            sum_copy(way, at).wait_send()


def body(ny, item_states, item_gain, hist_ids, lengths, attn_gain, w_q, w_kv, q_gain, k_gain, w_out):
    n_seq = lax.axis_size("seq")
    n_item = lax.axis_size("item")
    nq = n_seq // ny
    per_dev, width = item_states.shape
    rows = hist_ids.shape[0]
    share = rows // n_item
    far = n_item // 2
    span = LEN // rows
    chips = span // CORES
    out_cols = width // n_item
    q_cols = w_q.shape[1]
    group = q_cols // HD
    cols = width // PARTS
    tall = 2 * width // HD
    steps = 2 * far - 1
    dma = pltpu.SemaphoreType.DMA
    vmem, smem, hbm = (pl.BlockSpec(memory_space=space) for space in (pltpu.VMEM, pltpu.SMEM, pl.ANY))
    return pl.pallas_call(
        functools.partial(kernel, n_item, n_seq, ny),
        out_shape=jax.ShapeDtypeStruct((rows, out_cols), BF16),
        in_specs=[smem] + [hbm] * 9,
        out_specs=vmem,
        scratch_shapes=[
            pltpu.VMEM((1, rows), I32),
            pltpu.VMEM((per_dev, width), BF16),
            pltpu.VMEM((1, width), F32),
            pltpu.VMEM((1, width), F32),
            pltpu.VMEM((1, HD), F32),
            pltpu.VMEM((1, HD), F32),
            pltpu.VMEM((width, q_cols), BF16),
            pltpu.VMEM((width * 2, HD), BF16),
            pltpu.VMEM((width, 2 * HD), BF16),
            pltpu.VMEM((q_cols, width), BF16),
            pltpu.VMEM((PARTS, n_item, per_dev, cols), BF16),
            pltpu.VMEM((ny, nq, 128), I32),
            pltpu.VMEM((ny, nq, 128), I32),
            pltpu.VMEM((nq, ny, 128), I32),
            pltpu.VMEM((nq, ny, 128), I32),
            pltpu.VMEM((n_seq * tall, HD), F32),
            pltpu.VMEM((n_seq, tall, HD), BF16),
            pltpu.VMEM((n_seq, tall, HD), BF16),
            pltpu.VMEM((PARTS, n_item, share, cols), BF16),
            pltpu.VMEM((rows, rows), BF16),
            pltpu.VMEM((group * rows, HD), BF16),
            pltpu.VMEM((span, rows, 2 * HD), BF16),
            pltpu.VMEM((span, 8, rows), F32),
            pltpu.VMEM((group * rows, HD), F32),
            pltpu.VMEM((group * rows, HD), F32),
            pltpu.VMEM((group * rows, HD), F32),
            pltpu.VMEM((rows, q_cols), BF16),
            pltpu.VMEM((rows, out_cols), BF16),
            pltpu.VMEM((2, steps, rows // 2, out_cols), BF16),
            pltpu.VMEM((2, steps, rows // 2, out_cols), BF16),
            dma((9,)),
            dma((2, PARTS, far)), dma((2, PARTS, far)),
            dma((ny,)), dma((ny,)), dma((nq,)), dma((nq,)),
            dma((1,)), dma((1,)),
            dma((2, PARTS, far)), dma((2, PARTS, far)),
            dma((chips - 1, far + 1)), dma((chips - 1, far + 1)),
            dma((chips, far + 1)), dma((chips, far + 1)),
            dma((2, steps)), dma((2, steps)),
        ],
        compiler_params=pltpu.CompilerParams(
            collective_id=1, has_side_effects=True, vmem_limit_bytes=VMEM_LIMIT
        ),
        name="user_layer",
    )(
        lengths, hist_ids.reshape(1, rows), item_states,
        item_gain.reshape(1, width), attn_gain.reshape(1, width), q_gain.reshape(1, HD),
        k_gain.reshape(1, HD), w_q, w_kv.reshape(width * 2, HD), w_out,
    )


def solution(mesh):
    placed = (
        P(("item", "seq"), None),
        P(),
        P("seq"),
        P(),
        P(),
        P(None, "item"),
        P(None, None, "item"),
        P(),
        P(),
        P("item", None),
    )
    return jax.shard_map(
        functools.partial(body, NY),
        mesh=mesh, in_specs=placed, out_specs=P("seq", "item"), check_vma=False,
    )
```

```python
import functools

import jax
import jax.numpy as jnp
from jax import lax
from jax.experimental import pallas as pl
from jax.experimental.pallas import tpu as pltpu
from jax.sharding import PartitionSpec as P

HD = 128
LEN = 4096
CORES = 2
PARTS = 2
NY = 8
F32, BF16, I32 = jnp.float32, jnp.bfloat16, jnp.int32
VMEM_LIMIT = 61 * 1024 * 1024


def rms(x, gain):
    return x * lax.rsqrt(jnp.mean(x * x, axis=-1, keepdims=True) + 1e-06) * gain


def iota(shape, dim):
    return lax.broadcasted_iota(I32, shape, dim)


def onehot(mask):
    return jnp.where(mask, 1.0, 0.0).astype(BF16)


def dot(a, b):
    return jnp.dot(a, b, preferred_element_type=F32)


def signal(sem, **where):
    pl.semaphore_signal(sem, inc=1, device_id=where, device_id_type=pl.DeviceIdType.MESH)


def remote(src, dst, send, recv, **where):
    return pltpu.make_async_remote_copy(
        src_ref=src, dst_ref=dst, send_sem=send, recv_sem=recv,
        device_id=where, device_id_type=pl.DeviceIdType.MESH,
    )


class ZRing:
    def __init__(self, piece, send, recv, n):
        self.piece, self.send, self.recv, self.n = piece, send, recv, n
        self.far = n // 2
        self.me = lax.axis_index("item")

    def copy(self, way, part, hop, shard):
        step = 1 if way == 0 else self.n - 1
        ref = self.piece(part, shard, way if hop == self.far else None)
        at = (way, part, hop - 1)
        return remote(
            ref, ref, self.send.at[at], self.recv.at[at], item=lax.rem(self.me + step, self.n)
        )

    def shard(self, way, hop):
        return lax.rem(self.me + (self.n - hop if way == 0 else hop), self.n)

    def start(self, part):
        for way in range(2):
            self.copy(way, part, 1, self.me).start()

    def land(self, part, hop):
        for way in range(2):
            self.copy(way, part, hop, self.shard(way, hop)).wait_recv()
            if hop < self.far:
                self.copy(way, part, hop + 1, self.shard(way, hop)).start()

    def drain(self, parts):
        for part in range(parts):
            for hop in range(1, self.far + 1):
                for way in range(2):
                    self.copy(way, part, hop, self.shard(way, hop - 1)).wait_send()


def rank_of(ids_row, ids_col, per_dev, n_seq, axis):
    rows = ids_row.shape[1]
    owner_row = (ids_row // per_dev) & (n_seq - 1)
    owner_col = (ids_col // per_dev) & (n_seq - 1)
    lane, sub = iota((rows, rows), 1), iota((rows, rows), 0)
    if axis == 0:
        same = (owner_col == owner_row) & (sub < lane)
        less = owner_col < owner_row
    else:
        same = (owner_col == owner_row) & (lane < sub)
        less = owner_row < owner_col
    within = jnp.sum(jnp.where(same, 1.0, 0.0), axis=axis, keepdims=True).astype(I32)
    before = jnp.sum(jnp.where(less, 1.0, 0.0), axis=axis, keepdims=True).astype(I32)
    return before + within, within


def kernel(
    n_item, n_seq, ny, len_ref, ids_hbm, states_hbm, igain_hbm, again_hbm, qg_hbm, kg_hbm,
    wq_hbm, wkv_hbm, wout_hbm, out_ref, ids_row_ref, states_ref, igain_ref, again_ref, qg_ref, kg_ref,
    wq_ref, wkv_raw, wkv_ref, wout_ref, table, id_a, id_b, id_c, id_d, wide, parcel, landed,
    every, order, query, kv, bias, acc, top, total, attn_ref, res_ref, outgo, income,
    w_sem, t_send, t_recv, iy_send, iy_recv, ix_send, ix_recv, row_send, row_recv,
    z_send, z_recv, lane_send, lane_recv, pair_send, pair_recv, o_send, o_recv,
):
    nq = n_seq // ny
    far = n_item // 2
    me = lax.axis_index("item")
    my_seq = lax.axis_index("seq")
    core = lax.rem(my_seq, CORES)
    other = 1 - core
    sibling = my_seq + 1 - 2 * core
    my_y = lax.rem(my_seq // CORES, ny)
    my_x = my_seq // (CORES * ny)
    my_q = my_x * CORES + core
    per_dev, width = states_ref.shape
    rows = ids_row_ref.shape[1]
    share = rows // n_item
    span = LEN // rows
    chips = span // CORES
    chip = lax.rem(my_seq // CORES, chips)
    not_last = chip < chips - 1
    base = lax.rem(my_seq, span) * rows
    length = len_ref[my_seq // span]
    q_cols = wq_ref.shape[1]
    group = q_cols // HD
    out_cols = width // n_item
    parts = every.shape[0]
    cols = width // parts

    def along_y(y):
        return (my_x * ny + y) * CORES + core

    def along_q(q):
        return ((q // CORES) * ny + my_y) * CORES + lax.rem(q, CORES)

    def y_plus(d):
        return lax.rem(my_y + d, ny)

    def q_plus(d):
        return lax.rem(my_q + d, nq)

    n_mate = nq * ny
    my_mate = my_q * ny + my_y

    def mate_seq(m):
        q, y = m // ny, lax.rem(m, ny)
        return ((q // CORES) * ny + y) * CORES + lax.rem(q, CORES)

    def to_mates(do):
        def one(d, _):
            do(lax.rem(my_mate + d, n_mate))
            do(lax.rem(my_mate + n_mate - d, n_mate))
            return 0

        lax.fori_loop(1, n_mate // 2, one, 0)
        do(lax.rem(my_mate + n_mate // 2, n_mate))

    small = [(states_hbm, states_ref), (igain_hbm, igain_ref), (ids_hbm, ids_row_ref)]
    large = [(again_hbm, again_ref), (qg_hbm, qg_ref), (kg_hbm, kg_ref)]
    large += [(wq_hbm, wq_ref), (wkv_hbm, wkv_raw), (wout_hbm, wout_ref)]
    small, large = (
        [pltpu.make_async_copy(a, b, w_sem.at[at + i]) for i, (a, b) in enumerate(pairs)]
        for at, pairs in ((0, small), (len(small), large))
    )
    for copy in small + large:
        copy.start()

    barrier = pltpu.get_barrier_semaphore()
    for step in (1, n_item - 1):
        signal(barrier, item=lax.rem(me + step, n_item))
    to_mates(lambda m: signal(barrier, seq=mate_seq(m)))

    for copy in small:
        copy.wait()

    embed = rms(states_ref[...].astype(F32), igain_ref[...]).astype(BF16)
    for part in range(parts):
        table[part, me] = embed[:, part * cols:(part + 1) * cols]
    pl.semaphore_wait(barrier, 2 + n_mate - 1)

    def table_piece(part, shard, way):
        if way is None:
            return table.at[part, shard]
        return table.at[part, shard, pl.ds(way * (per_dev // 2), per_dev // 2)]

    items_ring = ZRing(table_piece, t_send, t_recv, n_item)
    for part in range(parts):
        items_ring.start(part)

    def land_items(hop):
        for part in range(parts):
            items_ring.land(part, hop)

    ids_row = ids_row_ref[...]
    diagonal = iota((rows, rows), 0) == iota((rows, rows), 1)
    ids_col = jnp.sum(jnp.where(diagonal, ids_row.astype(F32), 0.0), axis=1, keepdims=True).astype(I32)
    rank, within = rank_of(ids_row, ids_col, per_dev, n_seq, 0)
    owner = ids_row // per_dev
    owner_seq = owner & (n_seq - 1)
    source_y = (owner_seq // CORES) & (ny - 1)
    source_q = (owner_seq // (CORES * ny)) * CORES + (owner_seq & (CORES - 1))
    item = (owner // n_seq) * per_dev + (ids_row & (per_dev - 1)) + 1
    asks_at = rank & (n_item - 1)
    asks = asks_at == me
    copy_no = within // n_item
    place = jnp.where(asks, source_y * nq + source_q, -1)
    asked = []
    for sub in range(2):
        hit = (iota((ny * nq, rows), 0) == place) & (copy_no == sub)
        asked.append(jnp.sum(jnp.where(hit, item.astype(F32), 0.0), axis=1, keepdims=True).astype(I32))
    lanes = iota((ny * nq, 128), 1)
    id_a[...] = jnp.where(lanes == 0, asked[0], jnp.where(lanes == 1, asked[1], 0)).reshape(ny, nq, 128)

    def ids_y(d, y_from, y_to):
        return remote(
            id_a.at[y_to], id_b.at[y_from], iy_send.at[d - 1], iy_recv.at[d - 1], seq=along_y(y_to)
        )

    def ids_q(d, q_from, q_to):
        return remote(
            id_c.at[q_to], id_d.at[q_from], ix_send.at[d - 1], ix_recv.at[d - 1], seq=along_q(q_to)
        )

    for d in range(1, ny):
        ids_y(d, my_y, y_plus(d)).start()
    id_b[my_y] = id_a[my_y]

    spot = jnp.where(asks, rank // n_item, -1)
    pick_a = onehot(iota((share, rows), 0) == spot)
    sent = jnp.where(asks, copy_no * n_mate + source_q * ny + source_y, -1)
    pick_b = onehot(iota((2 * n_mate, rows), 0) == sent)
    pick = lax.dot_general(pick_a, pick_b, (((1,), (1,)), ((), ())), preferred_element_type=F32).astype(BF16)

    for d in range(1, ny):
        ids_y(d, y_plus(ny - d), my_y).wait_recv()
    for q in range(nq):
        id_c[q] = id_b[:, q, :]
    for d in range(1, nq):
        ids_q(d, my_q, q_plus(d)).start()
    id_d[my_q] = id_c[my_q]
    land_items(1)

    def landing(rank):
        apart = (rank - me + n_item) & (n_item - 1)
        place = jnp.where(apart == 0, 0, jnp.where(apart < far, 2 * apart, 2 * (n_item - apart) - 1))
        return place * share + rank // n_item

    goal_row = asks_at * share + rank // n_item
    pos_col = jnp.sum(
        jnp.where(goal_row == iota((rows, rows), 0), iota((rows, rows), 1).astype(F32), 0.0), axis=1, keepdims=True
    ).astype(I32)
    rank_col, _ = rank_of(ids_row, ids_col, per_dev, n_seq, 1)
    order[...] = onehot((rank_col & (n_item - 1)) * share + rank_col // n_item == iota((rows, rows), 1))
    placed = landing(rank_col) == iota((rows, rows), 1)
    pos_row = jnp.sum(jnp.where(placed, iota((rows, rows), 0).astype(F32), 0.0), axis=0, keepdims=True).astype(I32)
    bias[core] = jnp.broadcast_to(jnp.where(base + pos_row < length, 0.0, -jnp.inf), (8, rows))
    if far > 2:
        land_items(2)

    chunks = [slice(0, 3 * share if far > 1 else 2 * share)]
    for hop in range(2, far + 1):
        chunks.append(slice((2 * hop - 1) * share, min(2 * hop + 1, n_item) * share))
    n_chunks = len(chunks)

    def block(slot, c):
        if c < 0:
            return bias.at[slot]
        return kv.at[slot, pl.ds(chunks[c].start, chunks[c].stop - chunks[c].start)]

    def lane_copy(hop, c, far_off=False):
        return remote(
            block(core if far_off else (hop - 1) * 2 + core, c), block(hop * 2 + core, c),
            lane_send.at[hop - 1, c + 1], lane_recv.at[hop - 1, c + 1],
            seq=my_seq + (hop if far_off else 1) * CORES,
        )

    def pair_copy(hop, c, lane):
        return remote(
            block(hop * 2 + lane, c), block(hop * 2 + lane, c),
            pair_send.at[hop, c + 1], pair_recv.at[hop, c + 1], seq=sibling,
        )

    straight = range(n_chunks - 1, n_chunks)

    def give(c):
        if c in straight:
            for hop in range(1, chips):
                @pl.when(chip + hop < chips)
                def _():
                    lane_copy(hop, c, True).start()
        else:
            @pl.when(not_last)
            def _():
                lane_copy(1, c).start()

        @pl.when(core == 0)
        def _():
            pair_copy(0, c, 0).start()

    def take(hop, c):
        @pl.when(chip >= hop)
        def _():
            lane_copy(hop, c).wait_recv()
            if hop < chips - 1 and c not in straight:
                @pl.when(not_last)
                def _():
                    lane_copy(hop + 1, c).start()
            pair_copy(hop, c, core).start()

    def pass_on(stage):
        for hop in range(1, chips):
            for c in range(-1, n_chunks):
                if c not in straight and 2 * (c + 1) + hop == stage:
                    take(hop, c)

    give(-1)
    for hop in range(3, far):
        land_items(hop)
    for copy in large:
        copy.wait()
    strip = min(128, width)
    to, frm = iota((2 * strip, 2 * strip), 0), iota((2 * strip, 2 * strip), 1)
    split = onehot(frm == lax.rem(to, strip) * 2 + to // strip)
    for first in range(0, width, strip):
        both = dot(split, wkv_raw[first * 2:(first + strip) * 2]).astype(BF16)
        wkv_ref[first:first + strip, :HD] = both[:strip]
        wkv_ref[first:first + strip, HD:] = both[strip:]

    for d in range(1, nq):
        ids_q(d, q_plus(nq - d), my_q).wait_recv()
    wanted = id_d[...].reshape(nq * ny, 128)
    names = iota((nq * ny, n_item * per_dev), 1) + 1
    choose = [onehot(wanted[:, sub:sub + 1] == names) for sub in range(2)]
    blocks = width // HD
    tall = 2 * blocks

    def rows_copy(m_from, m_to):
        return remote(
            parcel.at[m_to], landed.at[m_from], row_send.at[0], row_recv.at[0], seq=mate_seq(m_to)
        )

    def all_but_one(buf, sem):
        ref = buf.at[pl.ds(0, n_mate - 1)]
        return pltpu.make_async_copy(ref, ref, sem.at[0])

    def rows_piece(part, shard, way):
        if way is None:
            return every.at[part, shard]
        return every.at[part, shard, pl.ds(way * (share // 2), share // 2)]

    ring = ZRing(rows_piece, z_send, z_recv, n_item)

    for part in range(parts):
        if far > 1:
            items_ring.land(part, far)
        source = table[part].reshape(n_item * per_dev, cols)
        for sub in range(2):
            picked = dot(choose[sub], source)
            for k in range(cols // HD):
                at = sub * blocks + part * (cols // HD) + k
                wide[pl.ds(at, n_mate, stride=tall), :] = picked[:, k * HD:(k + 1) * HD]
    parcel[...] = wide[...].reshape(n_mate, tall, HD).astype(BF16)
    to_mates(lambda m: rows_copy(my_mate, m).start())
    landed[my_mate] = parcel[my_mate]

    all_but_one(landed, row_recv).wait()
    wide[...] = landed[...].reshape(n_mate * tall, HD).astype(F32)
    for part in range(parts):
        for k in range(cols // HD):
            at = part * (cols // HD) + k
            came = jnp.concatenate(
                [wide[pl.ds(sub * blocks + at, n_mate, stride=tall), :] for sub in range(2)], axis=0
            ).astype(BF16)
            every[part, me, :, k * HD:(k + 1) * HD] = dot(pick, came).astype(BF16)
        ring.start(part)

    scale = 1.4426950408889634 / HD**0.5

    def project(hop):
        shards = [me] if hop == 0 else [ring.shard(0, hop)] + ([ring.shard(1, hop)] if hop < far else [])
        first = 0 if hop == 0 else (2 * hop - 1) * share
        here = slice(first, first + len(shards) * share)
        x = jnp.concatenate(
            [jnp.concatenate([every[part, j] for part in range(parts)], axis=1) for j in shards], axis=0
        )
        normed = rms(x.astype(F32), again_ref[...]).astype(BF16)
        q = dot(normed, wq_ref[...])
        key = dot(normed, wkv_ref[:, :HD])
        value = dot(normed, wkv_ref[:, HD:])
        for g in range(group):
            piece = rms(q[:, g * HD:(g + 1) * HD], qg_ref[...] * scale).astype(BF16)
            for at, j in enumerate(shards):
                there = pl.ds(pl.multiple_of(g * rows + j * share, share), share)
                query[there] = piece[at * share:(at + 1) * share]
        kv[core, here, :HD] = rms(key, kg_ref[...]).astype(BF16)
        kv[core, here, HD:] = value.astype(BF16)

    project(0)
    for hop in range(1, far + 1):
        ring.land(0, hop)
        pass_on(2 * hop - 1)
        ring.land(1, hop)
        project(hop)
        give(hop - 1)
        pass_on(2 * hop)

    def spread(x):
        return x[:, :rows] if rows < HD else jnp.concatenate([x] * (rows // HD), axis=1)

    def absorb(blocks, first):
        for g in range(group):
            here = slice(g * rows, (g + 1) * rows)
            q = query[here]
            if first:
                old = jnp.full((rows, HD), -1e30, F32)
            else:
                old, whole, out = top[here], total[here], acc[here]
            for slot in blocks:
                score = lax.dot_general(
                    q, kv[slot, :, :HD], (((1,), (1,)), ((), ())), preferred_element_type=F32
                ) + bias[slot, 0:1]
                if first:
                    score = jnp.where(pos_row <= pos_col, score, -jnp.inf)
                new = jnp.maximum(old, jnp.max(score, axis=-1, keepdims=True))
                weights = jnp.exp2(score - spread(new))
                part = jnp.sum(weights, axis=-1, keepdims=True)
                more = dot(weights.astype(BF16), kv[slot, :, HD:])
                if first:
                    whole, out = jnp.broadcast_to(part, (rows, HD)), more
                else:
                    shrink = jnp.exp2(old - new)
                    whole, out = whole * shrink + part, out * shrink + more
                old = new
            top[here], total[here], acc[here] = old, whole, out

    absorb([core], True)
    pass_on(2 * far + 1)
    take(1, straight[0])

    @pl.when(core == 1)
    def _():
        for c in range(-1, n_chunks):
            pair_copy(0, c, 0).wait_recv()
        absorb([0], False)

    for stage in range(2 * far + 2, 2 * far + chips):
        pass_on(stage)
    for hop in range(2, chips):
        take(hop, straight[0])
    for last in range(1, chips):
        @pl.when(chip == last)
        def _():
            for hop in range(1, last + 1):
                for c in range(-1, n_chunks):
                    pair_copy(hop, c, other).wait_recv()
            absorb([2 * hop + lane for hop in range(1, last + 1) for lane in range(2)], False)

    seen = jnp.concatenate(
        [(acc[g * rows:(g + 1) * rows] / total[g * rows:(g + 1) * rows]).astype(BF16) for g in range(group)], axis=1
    )
    fine = base + pos_col < length
    attn_ref[...] = jnp.where(fine, seen, jnp.zeros_like(seen))

    half_rows = rows // 2
    plan = []
    for way in range(2):
        steps = [(far, way)]
        for k in range(far - 1, 0, -1):
            steps += [(k, 1 - way), (k, way)]
        plan.append(steps)

    def partial(goal, half):
        here = pl.ds(pl.multiple_of(goal * out_cols, out_cols), out_cols)
        return dot(attn_ref[half * half_rows:(half + 1) * half_rows], wout_ref[:, here])

    def sum_copy(way, at):
        step = 1 if way == 0 else n_item - 1
        return remote(
            outgo.at[way, at], income.at[way, at], o_send.at[way, at], o_recv.at[way, at],
            item=lax.rem(me + step, n_item),
        )

    for at in range(len(plan[0])):
        for way in range(2):
            k, half = plan[way][at]
            goal = lax.rem(me + (k if way == 0 else n_item - k), n_item)
            value = partial(goal, half)
            if (k + 1, half) in plan[way]:
                before = plan[way].index((k + 1, half))
                sum_copy(way, before).wait_recv()
                value = value + income[way, before].astype(F32)
            outgo[way, at] = value.astype(BF16)
            sum_copy(way, at).start()
    where = me * out_cols
    inside = pl.ds(pl.multiple_of(lax.rem(where, cols), out_cols), out_cols)
    for half in (1, 0):
        here = slice(half * half_rows, (half + 1) * half_rows)
        first = half * (n_item // 2)
        own = every[where // cols, first:first + n_item // 2, :, inside].reshape(half_rows, out_cols)
        value = partial(me, half) + own.astype(F32)
        for way in range(2):
            if (1, half) in plan[way]:
                at = plan[way].index((1, half))
                sum_copy(way, at).wait_recv()
                value = value + income[way, at].astype(F32)
        res_ref[here] = value.astype(BF16)
    out_ref[...] = dot(order[...], res_ref[...]).astype(BF16)

    items_ring.drain(parts)
    ring.drain(parts)
    for d in range(1, ny):
        ids_y(d, my_y, y_plus(d)).wait_send()
    for d in range(1, nq):
        ids_q(d, my_q, q_plus(d)).wait_send()
    all_but_one(parcel, row_send).wait()
    for c in range(-1, n_chunks):
        @pl.when(core == 0)
        def _():
            pair_copy(0, c, 0).wait_send()

        for hop in range(1, chips):
            if c in straight:
                @pl.when(chip + hop < chips)
                def _():
                    lane_copy(hop, c, True).wait_send()
            else:
                @pl.when((chip >= hop - 1) & not_last)
                def _():
                    lane_copy(hop, c).wait_send()

            @pl.when(chip >= hop)
            def _():
                pair_copy(hop, c, core).wait_send()

    for way in range(2):
        for at in range(len(plan[0])):
            sum_copy(way, at).wait_send()


def body(ny, item_states, item_gain, hist_ids, lengths, attn_gain, w_q, w_kv, q_gain, k_gain, w_out):
    n_seq = lax.axis_size("seq")
    n_item = lax.axis_size("item")
    nq = n_seq // ny
    per_dev, width = item_states.shape
    rows = hist_ids.shape[0]
    share = rows // n_item
    far = n_item // 2
    span = LEN // rows
    chips = span // CORES
    out_cols = width // n_item
    q_cols = w_q.shape[1]
    group = q_cols // HD
    cols = width // PARTS
    tall = 2 * width // HD
    steps = 2 * far - 1
    dma = pltpu.SemaphoreType.DMA
    vmem, smem, hbm = (pl.BlockSpec(memory_space=space) for space in (pltpu.VMEM, pltpu.SMEM, pl.ANY))
    return pl.pallas_call(
        functools.partial(kernel, n_item, n_seq, ny),
        out_shape=jax.ShapeDtypeStruct((rows, out_cols), BF16),
        in_specs=[smem] + [hbm] * 9,
        out_specs=vmem,
        scratch_shapes=[
            pltpu.VMEM((1, rows), I32),
            pltpu.VMEM((per_dev, width), BF16),
            pltpu.VMEM((1, width), F32),
            pltpu.VMEM((1, width), F32),
            pltpu.VMEM((1, HD), F32),
            pltpu.VMEM((1, HD), F32),
            pltpu.VMEM((width, q_cols), BF16),
            pltpu.VMEM((width * 2, HD), BF16),
            pltpu.VMEM((width, 2 * HD), BF16),
            pltpu.VMEM((q_cols, width), BF16),
            pltpu.VMEM((PARTS, n_item, per_dev, cols), BF16),
            pltpu.VMEM((ny, nq, 128), I32),
            pltpu.VMEM((ny, nq, 128), I32),
            pltpu.VMEM((nq, ny, 128), I32),
            pltpu.VMEM((nq, ny, 128), I32),
            pltpu.VMEM((n_seq * tall, HD), F32),
            pltpu.VMEM((n_seq, tall, HD), BF16),
            pltpu.VMEM((n_seq, tall, HD), BF16),
            pltpu.VMEM((PARTS, n_item, share, cols), BF16),
            pltpu.VMEM((rows, rows), BF16),
            pltpu.VMEM((group * rows, HD), BF16),
            pltpu.VMEM((span, rows, 2 * HD), BF16),
            pltpu.VMEM((span, 8, rows), F32),
            pltpu.VMEM((group * rows, HD), F32),
            pltpu.VMEM((group * rows, HD), F32),
            pltpu.VMEM((group * rows, HD), F32),
            pltpu.VMEM((rows, q_cols), BF16),
            pltpu.VMEM((rows, out_cols), BF16),
            pltpu.VMEM((2, steps, rows // 2, out_cols), BF16),
            pltpu.VMEM((2, steps, rows // 2, out_cols), BF16),
            dma((9,)),
            dma((2, PARTS, far)), dma((2, PARTS, far)),
            dma((ny,)), dma((ny,)), dma((nq,)), dma((nq,)),
            dma((1,)), dma((1,)),
            dma((2, PARTS, far)), dma((2, PARTS, far)),
            dma((chips - 1, far + 1)), dma((chips - 1, far + 1)),
            dma((chips, far + 1)), dma((chips, far + 1)),
            dma((2, steps)), dma((2, steps)),
        ],
        compiler_params=pltpu.CompilerParams(
            collective_id=1, has_side_effects=True, vmem_limit_bytes=VMEM_LIMIT
        ),
        name="user_layer",
    )(
        lengths, hist_ids.reshape(1, rows), item_states,
        item_gain.reshape(1, width), attn_gain.reshape(1, width), q_gain.reshape(1, HD),
        k_gain.reshape(1, HD), w_q, w_kv.reshape(width * 2, HD), w_out,
    )


def solution(mesh):
    placed = (
        P(("item", "seq"), None),
        P(),
        P("seq"),
        P(),
        P(),
        P(None, "item"),
        P(None, None, "item"),
        P(),
        P(),
        P("item", None),
    )
    return jax.shard_map(
        functools.partial(body, NY),
        mesh=mesh, in_specs=placed, out_specs=P("seq", "item"), check_vma=False,
    )
```
